512 devices in a mesh: node: 32 (over y, x, core), period: 16 (over z).
Axes of the slice: x: 4, y: 4, z: 16, core: 2. Of those that a mesh axis runs over, the one named last changes fastest.
Arguments:
- prod_start: float32 [128, 131072], P('period', 'node'), may hold values from 0 to 1
- flow_inner_start: float32 [128, 655360], P('period', 'node'), may hold values from 0 to 1
- flow_cut_start: float32 [128, 131072], P('period', 'node'), may hold values from 0 to 1
- dual_start: float32 [128, 131072], P('period', 'node'), may hold values from -6 to 6
- cost_prod: float32 [128, 131072], P('period', 'node'), may hold values from 0.02 to 14
- cost_inner: float32 [128, 655360], P('period', 'node'), may hold values from 0.02 to 14
- cost_cut: float32 [128, 131072], P('period', 'node'), may hold values from 0.02 to 14
- inv_target: float32 [128, 131072], P('period', 'node'), may hold values from 0.04 to 27
- keep: float32 [128, 131072], P('period', 'node'), may hold values from 0.45 to 1
- inner_tail: int32 [655360], P('node'), may hold values from 0 to 4095, as said below
- inner_head: int32 [655360], P('node'), may hold values from 0 to 4095, as said below
- cut_tail: int32 [131072], P('node'), may hold values from 0 to 4095, as said below
- cut_head: int32 [131072], P('node'), may hold values from 0 to 4095, as said below
Outputs:
- prod_final: float32 [128, 131072], P('period', 'node')
- flow_inner_final: float32 [128, 655360], P('period', 'node')
- flow_cut_final: float32 [128, 131072], P('period', 'node')
- dual_final: float32 [128, 131072], P('period', 'node')
The draws below stay inside these ranges and needn't reach their ends.
Inputs may be any that keep to these rules, and one draw needn't show every extreme that they name: `inner_tail`: inner arcs come in aligned blocks of 128 within a slab; with j the block's number within its slab, R = 32, the tails of block j are the nodes of tile j % R (nodes (j % R) * 128 to (j % R) * 128 + 127), each once. `inner_head`: the heads of inner arc block j are the nodes of tile (j % R + j // R) % R, each once, with R = 32. `cut_tail`: cut tails of the entries m to m + 127 of a slab's list, m a multiple of 128, are the nodes m to m + 127 of the slab, each once. `cut_head`: cut heads of the entries m to m + 127 of a slab's list, m a multiple of 128, are the nodes m to m + 127 of the slab, each once.
All inputs are finite; a program needn't handle non-finite values.
Results may differ from the reference program's by a relative error of at most 0.00012.
Values sent between devices are 32-bit elements; how exact they have to be, the bound alone decides.
A program may use at most 64 MiB of HBM per device.

```python
import math
import jax
import jax.numpy as jnp
from jax import lax

SLAB = 4096
ITERS = 2
TILE = 128
INNER = 20480
CUT = 128
NETWORK_NODES = 131072
INNER_ALL = 655360
HORIZON_PERIODS = 128
N_NODE = 32


def ramped(key, row_count, column_count, lower, upper):
    key_base, key_scale = jax.random.split(key, 2)
    row_place = (jnp.arange(row_count, dtype=jnp.float32) / row_count)[:, None]
    column_place = (jnp.arange(column_count, dtype=jnp.float32) / column_count)[None, :]
    scale = jnp.exp(jax.random.uniform(key_scale, (1, column_count), jnp.float32, math.log(0.3), math.log(3.0)))
    base = jax.random.uniform(key_base, (row_count, column_count), jnp.float32, lower, upper)
    ramp = jnp.sqrt((1.0 + 2.0 * column_place) * (1.0 + 2.0 * row_place))
    return base * scale * ramp


def tile_offsets(key, block_count):
    scores = jax.random.randint(key, (block_count, TILE), 0, 1 << 20, dtype=jnp.int32)
    scores = scores * TILE + jnp.arange(TILE, dtype=jnp.int32)[None, :]
    return jnp.argsort(scores, axis=1).astype(jnp.int32)


def tiled_ends(key, entry_count, period_blocks, rolled):
    block_count = entry_count // TILE
    tile_count = SLAB // TILE
    numbers = jnp.arange(block_count, dtype=jnp.int32) % period_blocks
    tiles = numbers % tile_count
    if rolled:
        tiles = (tiles + numbers // tile_count) % tile_count
    return (tiles[:, None] * TILE + tile_offsets(key, block_count)).reshape(entry_count).astype(jnp.int32)


def draw_cost_prod(key, part):
    return ramped(jax.random.fold_in(key, 11), HORIZON_PERIODS, NETWORK_NODES, 0.25, 0.75)


def draw_cost_inner(key, part):
    return ramped(jax.random.fold_in(key, 12), HORIZON_PERIODS, INNER_ALL, 0.25, 0.75)


def draw_cost_cut(key, part):
    return ramped(jax.random.fold_in(key, 13), HORIZON_PERIODS, NETWORK_NODES, 0.25, 0.75)


def draw_inv_target(key, part):
    return ramped(jax.random.fold_in(key, 14), HORIZON_PERIODS, NETWORK_NODES, 0.5, 1.5)


def draw_keep(key, part):
    key_rapid, key_gradual, key_brisk, key_spike, key_removal = jax.random.split(jax.random.fold_in(key, 15), 5)
    share = 0.5
    fast = jax.random.uniform(key_rapid, (1, NETWORK_NODES), jnp.float32) < share
    slow_rate = jnp.exp(jax.random.uniform(key_gradual, (1, NETWORK_NODES), jnp.float32, math.log(0.05), math.log(1.5))) / HORIZON_PERIODS
    slow_rate = jnp.minimum(slow_rate, 0.1)
    fast_rate = jnp.exp(jax.random.uniform(key_brisk, (1, NETWORK_NODES), jnp.float32, math.log(1.0 / 50.0), math.log(1.0 / 30.0)))
    growth_rate = jnp.where(fast, fast_rate, slow_rate)
    spike_amount = jax.random.uniform(key_spike, (HORIZON_PERIODS, NETWORK_NODES), jnp.float32) < 3.0 / HORIZON_PERIODS
    removed_entries = jax.random.uniform(key_removal, (HORIZON_PERIODS, NETWORK_NODES), jnp.float32, 0.5, 0.8)
    return jnp.exp(-growth_rate) * jnp.where(spike_amount, removed_entries, 1.0)


def draw_inner_tail(key, part):
    return tiled_ends(jax.random.fold_in(key, 21), INNER_ALL, INNER // TILE, False)


def draw_inner_head(key, part):
    return tiled_ends(jax.random.fold_in(key, 22), INNER_ALL, INNER // TILE, True)


def draw_cut_tail(key, part):
    return tiled_ends(jax.random.fold_in(key, 23), NETWORK_NODES, SLAB // TILE, False)


def draw_cut_head(key, part):
    return tiled_ends(jax.random.fold_in(key, 24), NETWORK_NODES, SLAB // TILE, False)


def level_of(stream_key, extent, cuts, smallest, high):
    def one(dim, blocks):
        steps = jax.random.uniform(jax.random.fold_in(jax.random.fold_in(stream_key, 6), dim), (blocks,), jnp.float32, smallest / len(cuts), high / len(cuts))
        return jnp.repeat(jnp.exp(steps), extent[dim] // blocks).reshape((-1,) + (1,) * (len(extent) - dim - 1))

    level = one(*cuts[0])
    for cut in cuts[1:]:
        level = level * one(*cut)
    return level


def bell_draw(own_key, shape, deviation, bound, pieces=(), kind=jnp.bfloat16):
    entries = deviation * jax.random.normal(own_key, shape, jnp.float32)
    if pieces:
        entries = entries * level_of(own_key, shape, pieces, -0.22, 0.18)
    return jnp.clip(entries, -bound, bound).astype(kind)


def setup_inputs(seed: int = 0) -> dict:
    keys = jax.random.split(jax.random.key(seed), 14)
    prod_start = jnp.clip(1.0 * jax.random.uniform(keys[0], (HORIZON_PERIODS, NETWORK_NODES), jnp.float32) ** level_of(keys[0], (HORIZON_PERIODS, NETWORK_NODES), ((0, 16), (1, 32)), -0.2, 0.2), 0.0, 1.0)
    flow_inner_start = jnp.clip(1.0 * jax.random.uniform(keys[1], (HORIZON_PERIODS, INNER_ALL), jnp.float32) ** level_of(keys[1], (HORIZON_PERIODS, INNER_ALL), ((0, 16), (1, 32)), -0.2, 0.2), 0.0, 1.0)
    flow_cut_start = jnp.clip(1.0 * jax.random.uniform(keys[2], (HORIZON_PERIODS, NETWORK_NODES), jnp.float32) ** level_of(keys[2], (HORIZON_PERIODS, NETWORK_NODES), ((0, 16), (1, 32)), -0.2, 0.2), 0.0, 1.0)
    dual_start = bell_draw(keys[3], (HORIZON_PERIODS, NETWORK_NODES), 1.0, 6.0, ((0, 16), (1, 32)), jnp.float32)
    cost_prod = draw_cost_prod(jax.random.fold_in(keys[13], 71), 0)
    cost_inner = draw_cost_inner(jax.random.fold_in(keys[13], 71), 0)
    cost_cut = draw_cost_cut(jax.random.fold_in(keys[13], 71), 0)
    inv_target = draw_inv_target(jax.random.fold_in(keys[13], 71), 0)
    keep = draw_keep(jax.random.fold_in(keys[13], 71), 0)
    inner_tail = draw_inner_tail(jax.random.fold_in(keys[13], 71), 0)
    inner_head = draw_inner_head(jax.random.fold_in(keys[13], 71), 0)
    cut_tail = draw_cut_tail(jax.random.fold_in(keys[13], 71), 0)
    cut_head = draw_cut_head(jax.random.fold_in(keys[13], 71), 0)
    return dict(prod_start=prod_start, flow_inner_start=flow_inner_start, flow_cut_start=flow_cut_start, dual_start=dual_start, cost_prod=cost_prod, cost_inner=cost_inner, cost_cut=cost_cut, inv_target=inv_target, keep=keep, inner_tail=inner_tail, inner_head=inner_head, cut_tail=cut_tail, cut_head=cut_head)


ETA = 0.25

def stock_forward(net, keep):

    def advance(carry, pair):
        value, factor = pair
        carry = factor * carry + value
        return (carry, carry)
    _, stock = lax.scan(advance, jnp.zeros(net.shape[1:], jnp.float32), (net, keep))
    return stock

def price_backward(dual, keep):
    later = jnp.concatenate([keep[1:], jnp.zeros_like(keep[:1])], axis=0)

    def advance(carry, pair):
        value, factor = pair
        carry = value + factor * carry
        return (carry, carry)
    _, accumulated = lax.scan(advance, jnp.zeros(dual.shape[1:], jnp.float32), (dual, later), reverse=True)
    return accumulated

def reference(prod_start, flow_inner_start, flow_cut_start, dual_start, cost_prod, cost_inner, cost_cut, inv_target, keep, inner_tail, inner_head, cut_tail, cut_head):
    arcs = jnp.arange(INNER * N_NODE, dtype=jnp.int32)
    inner_base = arcs // INNER * SLAB
    tails_inner = inner_base + inner_tail
    heads_inner = inner_base + inner_head
    columns = jnp.arange(NETWORK_NODES, dtype=jnp.int32)
    source = columns // SLAB
    target_slab = columns % SLAB // CUT
    slot = columns % CUT
    tails_cut = source * SLAB + cut_tail
    heads_cut = target_slab * SLAB + cut_head[target_slab * SLAB + source * CUT + slot]

    def balance(produced, inner_flow, cut_flow):
        empty = jnp.zeros_like(produced)
        net = produced + empty.at[:, heads_inner].add(inner_flow) - empty.at[:, tails_inner].add(inner_flow)
        return net + empty.at[:, heads_cut].add(cut_flow) - empty.at[:, tails_cut].add(cut_flow)
    cost_squares = jnp.sum(cost_prod * cost_prod) + jnp.sum(cost_inner * cost_inner) + jnp.sum(cost_cut * cost_cut)
    target_squares = jnp.sum(inv_target * inv_target)
    omega = jnp.sqrt(cost_squares / target_squares)
    tau = ETA / omega
    sigma = ETA * omega
    produced, inner_flow, cut_flow, dual = (prod_start, flow_inner_start, flow_cut_start, dual_start)
    for sweep in range(ITERS):
        price = price_backward(dual, keep) / HORIZON_PERIODS
        inner_price = price[:, heads_inner] - price[:, tails_inner]
        cut_price = price[:, heads_cut] - price[:, tails_cut]
        new_prod = jnp.maximum(produced - tau * (cost_prod - price), 0.0)
        new_inner = jnp.maximum(inner_flow - tau * (cost_inner - inner_price), 0.0)
        new_cut = jnp.maximum(cut_flow - tau * (cost_cut - cut_price), 0.0)
        net = balance(2.0 * new_prod - produced, 2.0 * new_inner - inner_flow, 2.0 * new_cut - cut_flow)
        dual = dual + sigma * (inv_target - stock_forward(net, keep) / HORIZON_PERIODS)
        produced, inner_flow, cut_flow = (new_prod, new_inner, new_cut)
    return (produced, inner_flow, cut_flow, dual)
```

```python
import functools

import jax
import jax.numpy as jnp
from jax import lax
from jax.experimental import pallas as pl
from jax.experimental.pallas import tpu as pltpu
from jax.sharding import PartitionSpec as P

MESH = pl.DeviceIdType.MESH
ETA = 0.25
LANES = 128
ROWS = 8
PITCH = 16
PACK = 24
SENT = 18


def take(values, lanes):
    return jnp.take_along_axis(values, lanes, axis=1, mode="promise_in_bounds")


def sort_lanes(values):
    lane = lax.broadcasted_iota(jnp.int32, values.shape, 1)
    size = 2
    while size <= LANES:
        step = size // 2
        while step:
            other = take(values, lane ^ step)
            low = ((lane & size) == 0) == ((lane & step) == 0)
            values = jnp.where(low, jnp.minimum(values, other), jnp.maximum(values, other))
            step //= 2
        size *= 2
    return values


def kernel(sizes, *refs):
    nodes, periods, tiles, groups = sizes
    (
        prod_in, flow_in, cut_in, dual_in, cost_prod_in, cost_inner_in, cost_cut_in, target_in, keep_in,
        tail_in, head_in, cut_tail_in, cut_head_in,
        prod_out, flow_out, cut_out, dual_out,
        prod, flow, cut, dual, cost_prod, cost_inner, cost_cut, target, keep,
        tail, head, cut_tail, cut_head,
        kept, duals, targets, grown, price, price_late, net, change,
        keys, second, slot, ends_out, ends_in,
        pack, packs, flow_back, cost_back,
        swapped, swapped_late,
        send_a, recv_a, give_a, got_a,
        send_b, recv_b, give_b, got_b,
        send_c, recv_c, give_c, got_c,
        factor, square,
        in_sem, out_sem, send_sem, recv_sem,
    ) = refs
    me_node = lax.axis_index("node")
    me_period = lax.axis_index("period")
    horizon = periods * ROWS
    blocks = groups * tiles

    def tile(ref, number, pitch=ROWS):
        return ref[pl.ds(pl.multiple_of(number * pitch, ROWS), ROWS), :]

    def put(ref, number, values, pitch=ROWS):
        ref[pl.ds(pl.multiple_of(number * pitch, ROWS), ROWS), :] = values

    def lanes_of(ref, number):
        return jnp.broadcast_to(ref[pl.ds(number, 1), :], (ROWS, LANES))

    loads = [
        pltpu.make_async_copy(source, target_ref, in_sem.at[k])
        for k, (source, target_ref) in enumerate(
            (
                (keep_in, keep),
                (dual_in, dual),
                (cut_tail_in, cut_tail),
                (cut_head_in, cut_head),
                (cut_in, cut),
                (cost_cut_in, cost_cut),
                (tail_in, tail),
                (head_in, head),
                (target_in, target),
                (cost_prod_in, cost_prod),
                (cost_inner_in, cost_inner),
                (flow_in, flow),
                (prod_in, prod),
            )
        )
    ]
    for load in loads:
        load.start()

    barrier = pltpu.get_barrier_semaphore()

    def greet_period(k, _):
        pl.semaphore_signal(
            barrier, inc=1, device_id={"period": lax.rem(me_period + k, periods)}, device_id_type=MESH
        )
        return 0

    def greet_node(k, _):
        pl.semaphore_signal(
            barrier, inc=1, device_id={"node": lax.rem(me_node + k, nodes)}, device_id_type=MESH
        )
        return 0

    lax.fori_loop(1, periods, greet_period, 0)
    lax.fori_loop(1, nodes, greet_node, 0)

    def period_copy(source, target_ref, rows, phase, k):
        peer = lax.rem(me_period + k, periods)
        return pltpu.make_async_remote_copy(
            src_ref=source.at[pl.ds(pl.multiple_of(peer * ROWS, ROWS), rows), :],
            dst_ref=target_ref.at[pl.ds(pl.multiple_of(me_period * ROWS, ROWS), rows), :],
            send_sem=send_sem.at[phase],
            recv_sem=recv_sem.at[phase],
            device_id={"period": peer},
            device_id_type=MESH,
        )

    def node_copy(source, target_ref, pitch, rows, phase, k):
        peer = lax.rem(me_node + k, nodes)
        return pltpu.make_async_remote_copy(
            src_ref=source.at[pl.ds(pl.multiple_of(peer * pitch, ROWS), rows), :],
            dst_ref=target_ref.at[pl.ds(pl.multiple_of(me_node * pitch, ROWS), rows), :],
            send_sem=send_sem.at[phase],
            recv_sem=recv_sem.at[phase],
            device_id={"node": peer},
            device_id_type=MESH,
        )

    def spread_periods(source, target_ref, rows, phase):
        def one(k, _):
            period_copy(source, target_ref, rows, phase, k).start()
            return 0

        lax.fori_loop(1, periods, one, 0)
        put(target_ref, me_period, tile(source, me_period))

    def spread_nodes(source, target_ref, pitch, rows, phase):
        def one(k, _):
            node_copy(source, target_ref, pitch, rows, phase, k).start()
            return 0

        lax.fori_loop(1, nodes, one, 0)
        for part in range(pitch // ROWS):
            at = pl.ds(pl.multiple_of(me_node * pitch + part * ROWS, ROWS), ROWS)
            target_ref[at, :] = source[at, :]

    def await_rows(ref, rows, semaphore):
        whole = ref.at[pl.ds(0, rows), :]
        pltpu.make_async_copy(whole, whole, semaphore).wait()

    def arrived_periods(target_ref, rows, phase):
        await_rows(target_ref, (periods - 1) * rows, recv_sem.at[phase])

    def arrived_nodes(target_ref, rows, phase):
        await_rows(target_ref, (nodes - 1) * rows, recv_sem.at[phase])

    half = tiles // 2

    def put_summary(ref, row, values):
        ref[pl.ds(row, half, stride=ROWS), :] = values[:half]
        ref[pl.ds(row + 1, half, stride=ROWS), :] = values[half:]

    def get_summary(ref, row):
        return jnp.concatenate(
            [ref[pl.ds(row, half, stride=ROWS), :], ref[pl.ds(row + 1, half, stride=ROWS), :]], axis=0
        )

    def at_period(ref, t):
        return ref[pl.ds(t * tiles, tiles), :]

    row_number = lax.broadcasted_iota(jnp.int32, (ROWS, LANES), 0)
    none = jnp.zeros((ROWS, LANES), jnp.float32)

    loads[0].wait()
    loads[1].wait()
    product = None
    square_sum = None
    for t in range(ROWS):
        share = keep[pl.ds(t, tiles, stride=ROWS), :]
        kept[pl.ds(t * tiles, tiles), :] = share
        product = share if product is None else product * share
        grown[pl.ds(t * tiles, tiles), :] = product
        square_sum = product * product if square_sum is None else square_sum + product * product
    passed = None
    for t in reversed(range(ROWS)):
        value = dual[pl.ds(t, tiles, stride=ROWS), :]
        duals[pl.ds(t * tiles, tiles), :] = value
        passed = value if passed is None else value + passed
        passed = passed * at_period(kept, t)
    put_summary(send_a, 0, product)
    put_summary(send_a, 2, passed)
    put_summary(send_a, 4, square_sum)

    for k in (2, 3, 4, 5):
        loads[k].wait()

    def pack_one(d, _):
        put(pack, d, tile(cut, d), PACK)
        pack[pl.ds(pl.multiple_of(d * PACK + ROWS, ROWS), ROWS), :] = tile(cost_cut, d)
        return 0

    lax.fori_loop(0, nodes, pack_one, 0)
    cut_tail[...] = cut_tail[...] & (LANES - 1)
    cut_head[...] = cut_head[...] & (LANES - 1)
    pack[pl.ds(2 * ROWS, nodes, stride=PACK), :] = cut_tail[...].astype(jnp.float32)
    pack[pl.ds(2 * ROWS + 1, nodes, stride=PACK), :] = cut_head[...].astype(jnp.float32)

    pl.semaphore_wait(barrier, periods + nodes - 2)
    spread_periods(send_a, recv_a, 6, 0)
    spread_nodes(pack, packs, PACK, SENT, 6)

    for k in (8, 9, 10):
        loads[k].wait()

    def square_one(t, sums):
        costs, wanted = sums
        value = tile(target, t)
        wanted = wanted + value * value
        value = tile(cost_prod, t)
        costs = costs + value * value
        value = tile(cost_cut, t)
        costs = costs + value * value
        for group in range(groups):
            value = tile(cost_inner, group * tiles + t)
            costs = costs + value * value
        return costs, wanted

    costs, wanted = lax.fori_loop(0, tiles, square_one, (none, none))
    costs = jnp.sum(costs, axis=0, keepdims=True)
    wanted = jnp.sum(wanted, axis=0, keepdims=True)

    arrived_periods(recv_a, 6, 0)
    entering = none
    for j in reversed(range(periods)):
        block = tile(recv_a, j)
        ratio = jnp.where(row_number < 2, block, pltpu.roll(block, 2, 0))
        put(factor, j, ratio)
        put(square, j, pltpu.roll(block, ROWS - 2, 0))
        put(give_a, j, jnp.where(row_number < 1, costs, jnp.where(row_number < 2, wanted, entering)))
        entering = block + ratio * entering
    spread_periods(give_a, got_a, 4, 1)

    loads[6].wait()
    loads[7].wait()
    tail[...] = tail[...] & (LANES - 1)
    head[...] = head[...] & (LANES - 1)

    def keyed(first, other):
        lane = lax.broadcasted_iota(jnp.int32, first.shape, 1)
        return (first * (LANES * LANES) + other * LANES + lane).astype(jnp.float32)

    keys[pl.ds(0, blocks), :] = keyed(tail[...], head[...])
    keys[pl.ds(blocks, blocks), :] = keyed(head[...], tail[...])
    keys[pl.ds(2 * blocks, nodes), :] = keyed(cut_tail[...], cut_head[...])
    keys[pl.ds(2 * blocks + nodes, nodes), :] = keyed(cut_head[...], cut_tail[...])
    batch = 128

    def sort_batch(k, _):
        at = pl.ds(pl.multiple_of(k * batch, batch), batch)
        ordered = sort_lanes(keys[at, :]).astype(jnp.int32)
        second[at, :] = lax.shift_right_logical(ordered, 7) & (LANES - 1)
        slot[at, :] = ordered & (LANES - 1)
        return 0

    lax.fori_loop(0, (2 * blocks + 2 * nodes) // batch, sort_batch, 0)

    loads[11].wait()
    loads[12].wait()

    def reorder(t, _):
        for group in range(groups):
            j = group * tiles + t
            lanes = lanes_of(slot, j)
            put(flow, j, take(tile(flow, j), lanes))
            put(cost_inner, j, take(tile(cost_inner, j), lanes))
        lanes = lanes_of(slot, 2 * blocks + t)
        put(cut, t, take(tile(cut, t), lanes))
        put(cost_cut, t, take(tile(cost_cut, t), lanes))
        return 0

    lax.fori_loop(0, tiles, reorder, 0)

    for t in range(ROWS):
        targets[pl.ds(t * tiles, tiles), :] = target[pl.ds(t, tiles, stride=ROWS), :]

    arrived_periods(got_a, 4, 1)
    entering = get_summary(got_a, 2)
    for t in reversed(range(ROWS)):
        entering = at_period(duals, t) + entering
        price[pl.ds(t, tiles, stride=PITCH), :] = entering * (1.0 / horizon)
        entering = entering * at_period(kept, t)
    for row in range(2):
        column = jnp.sum(got_a[pl.ds(row, periods, stride=ROWS), :], axis=0, keepdims=True)
        price[pl.ds(ROWS + row, tiles, stride=PITCH), :] = jnp.broadcast_to(column, (tiles, LANES))
    spread_nodes(price, swapped, PITCH, ROWS + 2, 7)

    arrived_nodes(packs, SENT, 6)
    ends_out[...] = take(
        packs[pl.ds(2 * ROWS + 1, nodes, stride=PACK), :], slot[pl.ds(2 * blocks, nodes), :]
    ).astype(jnp.int32)
    ends_in[...] = take(
        packs[pl.ds(2 * ROWS, nodes, stride=PACK), :], slot[pl.ds(2 * blocks + nodes, nodes), :]
    ).astype(jnp.int32)

    def reorder_back(d, _):
        lanes = lanes_of(slot, 2 * blocks + nodes + d)
        put(flow_back, d, take(tile(packs, d, PACK), lanes))
        at = pl.ds(pl.multiple_of(d * PACK + ROWS, ROWS), ROWS)
        put(cost_back, d, take(packs[at, :], lanes))
        return 0

    lax.fori_loop(0, nodes, reorder_back, 0)

    def update_inner(prices, tau):
        def one(t, _):
            here = tile(prices, t, PITCH)
            old = tile(prod, t)
            new = jnp.maximum(old - tau * (tile(cost_prod, t) - here), 0.0)
            put(prod, t, new)
            total = 2.0 * new - old
            for group in range(groups):
                j = group * tiles + t
                there = take(tile(prices, lax.rem(t + group, tiles), PITCH), lanes_of(second, j))
                old = tile(flow, j)
                new = jnp.maximum(old - tau * (tile(cost_inner, j) - (there - here)), 0.0)
                put(flow, j, new)
                moved = 2.0 * new - old
                put(change, j, moved)
                total = total - moved
            put(net, t, total)
            return 0

        lax.fori_loop(0, tiles, one, 0)

    def update_cut(prices, others, tau):
        def one(t, _):
            here = tile(prices, t, PITCH)
            other = tile(others, t, PITCH)
            total = tile(net, t)
            there = take(other, lanes_of(ends_out, t))
            old = tile(cut, t)
            new = jnp.maximum(old - tau * (tile(cost_cut, t) - (there - here)), 0.0)
            put(cut, t, new)
            total = total - (2.0 * new - old)
            there = take(other, lanes_of(ends_in, t))
            old = tile(flow_back, t)
            new = jnp.maximum(old - tau * (tile(cost_back, t) - (here - there)), 0.0)
            put(flow_back, t, new)
            total = total + (2.0 * new - old)
            for group in range(groups):
                j = group * tiles + lax.rem(t - group + tiles, tiles)
                total = total + take(tile(change, j), lanes_of(second, blocks + j))
            put(net, t, total)
            return 0

        lax.fori_loop(0, tiles, one, 0)

    arrived_nodes(swapped, ROWS + 2, 7)
    sums = [
        jnp.sum(swapped[pl.ds(ROWS + row, nodes, stride=PITCH), :], keepdims=True) for row in range(2)
    ]
    omega = jnp.sqrt(sums[0] / sums[1])
    tau = jnp.broadcast_to(ETA / omega, (ROWS, LANES))
    sigma = ETA * omega
    sigma_tile = jnp.broadcast_to(sigma, (ROWS, LANES)) * (1.0 / horizon)
    sigma_wide = jnp.broadcast_to(sigma, (tiles, LANES))
    update_inner(price, tau)
    update_cut(price, swapped, tau)

    stock = None
    for t in range(ROWS):
        value = net[pl.ds(t, tiles, stride=ROWS), :]
        stock = value if stock is None else at_period(kept, t) * stock + value
        duals[pl.ds(t * tiles, tiles), :] = at_period(duals, t) + sigma_wide * (
            at_period(targets, t) - stock * (1.0 / horizon)
        )
    passed = None
    for t in reversed(range(ROWS)):
        value = at_period(duals, t)
        passed = value if passed is None else value + passed
        passed = passed * at_period(kept, t)
    put_summary(send_b, 0, stock)
    put_summary(send_b, 2, passed)
    spread_periods(send_b, recv_b, 4, 2)
    arrived_periods(recv_b, 4, 2)
    parts = [tile(recv_b, j) for j in range(periods)]
    entering = none
    entered = []
    for j in range(periods):
        entered.append(entering)
        entering = parts[j] + tile(factor, j) * entering
    entering = none
    for j in reversed(range(periods)):
        put(give_b, j, jnp.where(row_number < 2, entered[j], entering))
        answer = parts[j] - sigma_tile * tile(square, j) * pltpu.roll(entered[j], 2, 0)
        entering = answer + tile(factor, j) * entering
    spread_periods(give_b, got_b, 4, 3)
    arrived_periods(got_b, 4, 3)
    stock = get_summary(got_b, 0) * (sigma_wide * (1.0 / horizon))
    entering = get_summary(got_b, 2)
    for t in reversed(range(ROWS)):
        value = at_period(duals, t) - at_period(grown, t) * stock
        duals[pl.ds(t * tiles, tiles), :] = value
        entering = value + entering
        price_late[pl.ds(t, tiles, stride=PITCH), :] = entering * (1.0 / horizon)
        entering = entering * at_period(kept, t)

    spread_nodes(price_late, swapped_late, PITCH, ROWS, 8)
    update_inner(price_late, tau)
    arrived_nodes(swapped_late, ROWS, 8)
    update_cut(price_late, swapped_late, tau)
    stock = None
    for t in range(ROWS):
        value = net[pl.ds(t, tiles, stride=ROWS), :]
        stock = value if stock is None else at_period(kept, t) * stock + value
        duals[pl.ds(t * tiles, tiles), :] = at_period(duals, t) + sigma_wide * (
            at_period(targets, t) - stock * (1.0 / horizon)
        )
    put_summary(send_c, 0, stock)
    spread_periods(send_c, recv_c, 2, 4)
    store_prod = pltpu.make_async_copy(prod, prod_out, out_sem.at[0])
    store_prod.start()
    arrived_periods(recv_c, 2, 4)
    entering = none
    for j in range(periods):
        put(give_c, j, entering)
        entering = tile(recv_c, j) + tile(factor, j) * entering
    spread_periods(give_c, got_c, 2, 5)

    def restore(t, _):
        for group in range(groups):
            j = group * tiles + t
            put(flow, j, take(tile(flow, j), lanes_of(tail, j)))
        put(cut, t, take(tile(cut, t), lanes_of(cut_tail, t)))
        return 0

    lax.fori_loop(0, tiles, restore, 0)
    store_flow = pltpu.make_async_copy(flow, flow_out, out_sem.at[1])
    store_flow.start()
    store_cut = pltpu.make_async_copy(cut, cut_out, out_sem.at[2])
    store_cut.start()

    arrived_periods(got_c, 2, 5)
    stock = get_summary(got_c, 0) * (sigma_wide * (1.0 / horizon))
    for t in range(ROWS):
        dual[pl.ds(t, tiles, stride=ROWS), :] = at_period(duals, t) - at_period(grown, t) * stock
    store_dual = pltpu.make_async_copy(dual, dual_out, out_sem.at[3])
    store_dual.start()

    for phase, (ref, rows) in enumerate(
        ((send_a, 6), (give_a, 4), (send_b, 4), (give_b, 4), (send_c, 2), (give_c, 2))
    ):
        await_rows(ref, (periods - 1) * rows, send_sem.at[phase])
    for phase, ref, rows in ((6, pack, SENT), (7, price, ROWS + 2), (8, price_late, ROWS)):
        await_rows(ref, (nodes - 1) * rows, send_sem.at[phase])
    for store in (store_prod, store_flow, store_cut, store_dual):
        store.wait()


def solution(mesh):
    nodes, periods = mesh.shape["node"], mesh.shape["period"]

    def to_tiles(values):
        rows, columns = values.shape
        return values.reshape(rows, columns // LANES, LANES).transpose(1, 0, 2).reshape(-1, LANES)

    def from_tiles(values):
        count = values.shape[0] // ROWS
        return values.reshape(count, ROWS, LANES).transpose(1, 0, 2).reshape(ROWS, count * LANES)

    def body(*operands):
        floats = [to_tiles(values) for values in operands[:9]]
        indices = [values.reshape(-1, LANES) for values in operands[9:]]
        tiles = floats[0].shape[0] // ROWS
        groups = floats[1].shape[0] // floats[0].shape[0]
        blocks = tiles * groups
        slab = (tiles * ROWS, LANES)
        arcs = (blocks * ROWS, LANES)
        ring = (periods * ROWS, LANES)

        def room(shape, kind=jnp.float32):
            return pltpu.VMEM(shape, kind)

        scratch = [
            room(slab), room(arcs), room(slab), room(slab), room(slab), room(arcs), room(slab), room(slab), room(slab),
            room((blocks, LANES), jnp.int32), room((blocks, LANES), jnp.int32),
            room((tiles, LANES), jnp.int32), room((tiles, LANES), jnp.int32),
            room(slab), room(slab), room(slab), room(slab),
            room((tiles * PITCH, LANES)), room((tiles * PITCH, LANES)), room(slab), room(arcs),
            room((2 * blocks + 2 * nodes, LANES)),
            room((2 * blocks + 2 * nodes, LANES), jnp.int32), room((2 * blocks + 2 * nodes, LANES), jnp.int32),
            room((nodes, LANES), jnp.int32), room((nodes, LANES), jnp.int32),
            room((nodes * PACK, LANES)), room((nodes * PACK, LANES)), room(slab), room(slab),
            room((nodes * PITCH, LANES)), room((nodes * PITCH, LANES)),
        ] + [room(ring)] * 14 + [
            pltpu.SemaphoreType.DMA((13,)),
            pltpu.SemaphoreType.DMA((4,)),
            pltpu.SemaphoreType.DMA((9,)),
            pltpu.SemaphoreType.DMA((9,)),
        ]
        anywhere = pl.BlockSpec(memory_space=pl.ANY)
        outputs = pl.pallas_call(
            functools.partial(kernel, (nodes, periods, tiles, groups)),
            out_shape=[jax.ShapeDtypeStruct(shape, jnp.float32) for shape in (slab, arcs, slab, slab)],
            in_specs=[anywhere] * 13,
            out_specs=[anywhere] * 4,
            scratch_shapes=scratch,
            compiler_params=pltpu.CompilerParams(
                collective_id=0, has_side_effects=True, vmem_limit_bytes=32 * 1024 * 1024
            ),
        )(*floats, *indices)
        return tuple(from_tiles(values) for values in outputs)

    both, node = P("period", "node"), P("node")
    return jax.shard_map(
        body,
        mesh=mesh,
        in_specs=(both,) * 9 + (node,) * 4,
        out_specs=(both,) * 4,
        check_vma=False,
    )
```

```python
import functools

import jax
import jax.numpy as jnp
from jax import lax
from jax.experimental import pallas as pl
from jax.experimental.pallas import tpu as pltpu
from jax.sharding import PartitionSpec as P

MESH = pl.DeviceIdType.MESH
ETA = 0.25
LANES = 128
ROWS = 8
PACK = 40
SENT = 34
UNROLL = 4
LIMIT = 56 * 1024 * 1024


def take(values, lanes):
    return jnp.take_along_axis(values, lanes, axis=1, mode="promise_in_bounds")


def sort_lanes(values):
    lane = lax.broadcasted_iota(jnp.int32, values.shape, 1)
    size = 2
    while size <= LANES:
        step = size // 2
        while step:
            other = take(values, lane ^ step)
            low = ((lane & size) == 0) == ((lane & step) == 0)
            values = jnp.where(low, jnp.minimum(values, other), jnp.maximum(values, other))
            step //= 2
        size *= 2
    return values


def kernel(sizes, *refs):
    nodes, periods, tiles, groups = sizes
    (
        prod_in, flow_in, cut_in, dual_in, cost_prod_in, cost_inner_in, cost_cut_in, target_in, keep_in,
        tail_in, head_in, cut_tail_in, cut_head_in,
        prod, flow, cut, dual,
        cost_prod, cost_inner, cost_cut, target, keep,
        tail, head, cut_tail, cut_head,
        kept, duals, targets, grown, kept_far, grown_far,
        price, price_far, net, change,
        keys, second, slot, ends_out, ends_in,
        pack, packs, flow_back, cost_back,
        late, lates, part, parts,
        send_a, recv_a, give_a, got_a, far_a, send_s, recv_s,
        send_b, recv_b, give_b, got_b, far_b,
        send_c, recv_c, give_c, got_c,
        factor, factor_c,
        in_sem, send_sem, recv_sem,
    ) = refs
    me_node = lax.axis_index("node")
    me_period = lax.axis_index("period")
    horizon = periods * ROWS
    blocks = groups * tiles
    chunks = periods // 2
    reach = chunks // 2
    ranks = tiles // chunks
    me_chunk = lax.rem(me_period, chunks)

    def rows_at(number, rows=ROWS, pitch=ROWS):
        return pl.ds(pl.multiple_of(number * pitch, ROWS), rows)

    def tile(ref, number):
        return ref[rows_at(number), :]

    def put(ref, number, values):
        ref[rows_at(number), :] = values

    def lanes_of(ref, number):
        return jnp.broadcast_to(ref[pl.ds(number, 1), :], (ROWS, LANES))

    loads = [
        pltpu.make_async_copy(source, target_ref, in_sem.at[k])
        for k, (source, target_ref) in enumerate(
            (
                (keep_in, keep),
                (dual_in, dual),
                (cut_tail_in, cut_tail),
                (cut_head_in, cut_head),
                (cut_in, cut),
                (cost_cut_in, cost_cut),
                (tail_in, tail),
                (head_in, head),
                (target_in, target),
                (cost_prod_in, cost_prod),
                (cost_inner_in, cost_inner),
                (flow_in, flow),
                (prod_in, prod),
            )
        )
    ]
    for load in loads:
        load.start()

    def greet(device):
        pl.semaphore_signal(
            pltpu.get_barrier_semaphore(), inc=1, device_id=device, device_id_type=MESH
        )

    def greet_period(k, _):
        greet({"period": lax.rem(me_period + k, periods)})
        return 0

    def greet_node(k, _):
        greet({"node": lax.rem(me_node + k, nodes)})
        return 0

    node_chunk = lax.rem(me_node, chunks)
    source_plane = node_chunk + chunks * (
        lax.rem(me_period + periods + reach - node_chunk, periods) // chunks
    )

    def greet_far(k, _):
        greet({"node": lax.rem(me_node + k, nodes), "period": source_plane})
        return 0

    lax.fori_loop(1, periods, greet_period, 0)
    lax.fori_loop(1, nodes, greet_node, 0)
    lax.fori_loop(1, nodes, greet_far, 0)
    far_count = jnp.where(me_chunk == node_chunk, ranks - 1, ranks) * chunks

    def start(source, target_ref, source_rows, target_rows, phase, device):
        pltpu.make_async_remote_copy(
            src_ref=source.at[source_rows, :],
            dst_ref=target_ref.at[target_rows, :],
            send_sem=send_sem.at[phase],
            recv_sem=recv_sem.at[phase],
            device_id=device,
            device_id_type=MESH,
        ).start()

    def spread_owners(source, target_ref, rows, phase):
        def one(k, _):
            peer = lax.rem(me_period + k, periods)
            start(
                source, target_ref, rows_at(lax.rem(peer, chunks), rows), rows_at(me_period, rows), phase,
                {"period": peer},
            )
            return 0

        lax.fori_loop(1, periods, one, 0)
        put(target_ref, me_period, tile(source, me_chunk))

    def served(i):
        return lax.rem(me_period + periods - reach + i, periods)

    def give_back(source, target_ref, rows, phase):
        def one(i, _):
            @pl.when(i != reach)
            def _():
                peer = served(i)
                start(
                    source, target_ref, rows_at(peer, rows), rows_at(me_chunk, rows), phase,
                    {"period": peer},
                )

            return 0

        lax.fori_loop(0, chunks, one, 0)
        put(target_ref, me_chunk, tile(source, me_period))

    def give_far(source, target_ref, phase):
        for rank in range(ranks):
            to = me_chunk + rank * chunks

            @pl.when(to != me_node)
            def _():
                def one(i, _):
                    peer = served(i)
                    start(
                        source, target_ref,
                        pl.ds(pl.multiple_of(peer * ROWS, ROWS) + 2 * rank, 2), rows_at(me_node, 2), phase,
                        {"node": to, "period": peer},
                    )
                    return 0

                lax.fori_loop(0, chunks, one, 0)

    def spread_nodes(source, target_ref, pitch, rows, phase, same=False):
        def one(k, _):
            peer = lax.rem(me_node + k, nodes)
            start(
                source, target_ref, rows_at(0 if same else peer, rows, pitch), rows_at(me_node, rows, pitch), phase,
                {"node": peer},
            )
            return 0

        lax.fori_loop(1, nodes, one, 0)

    def await_rows(ref, rows, semaphore):
        whole = ref.at[pl.ds(0, rows), :]
        pltpu.make_async_copy(whole, whole, semaphore).wait()

    def put_summary(ref, row, values, pitch=2):
        for rank in range(ranks):
            ref[pl.ds(pitch * rank + row, chunks, stride=ROWS), :] = values[
                rank * chunks : (rank + 1) * chunks
            ]

    def get_summary(ref, row, pitch=2):
        return jnp.concatenate(
            [ref[pl.ds(pitch * rank + row, chunks, stride=ROWS), :] for rank in range(ranks)], axis=0
        )

    def at_period(ref, t):
        return ref[pl.ds(t * tiles, tiles), :]

    def by_node(ref, t, pitch=ROWS):
        return ref[pl.ds(t, tiles, stride=pitch), :]

    def chain_back(values, shares, entering, target_ref):
        for t in reversed(range(ROWS)):
            entering = values(t) + entering
            target_ref[pl.ds(t, tiles, stride=ROWS), :] = entering * (1.0 / horizon)
            entering = entering * at_period(shares, t)

    def passed_back():
        passed = None
        for t in reversed(range(ROWS)):
            value = at_period(duals, t)
            passed = value if passed is None else value + passed
            passed = passed * at_period(kept, t)
        return passed

    def products(share_of, shares, target_ref):
        product = None
        square_sum = None
        for t in range(ROWS):
            share = share_of(t)
            shares[pl.ds(t * tiles, tiles), :] = share
            product = share if product is None else product * share
            target_ref[pl.ds(t * tiles, tiles), :] = product
            square = product * product
            square_sum = square if square_sum is None else square_sum + square
        return product, square_sum

    even = (lax.broadcasted_iota(jnp.int32, (ROWS, LANES), 0) & 1) == 0
    none = jnp.zeros((ROWS, LANES), jnp.float32)

    loads[0].wait()
    loads[1].wait()
    product, square_sum = products(lambda t: by_node(keep, t), kept, grown)
    for t in range(ROWS):
        duals[pl.ds(t * tiles, tiles), :] = by_node(dual, t)
    put_summary(send_a, 0, product)
    put_summary(send_a, 1, passed_back())
    put_summary(send_s, 1, square_sum)

    for k in (2, 3, 4, 5):
        loads[k].wait()

    def pack_one(step, _):
        for k in range(UNROLL):
            d = step * UNROLL + k
            for place, ref in enumerate((cut, cost_cut, keep, dual)):
                pack[rows_at(d * (PACK // ROWS) + place), :] = tile(ref, d)
        return 0

    lax.fori_loop(0, nodes // UNROLL, pack_one, 0)
    cut_tail[...] = cut_tail[...] & (LANES - 1)
    cut_head[...] = cut_head[...] & (LANES - 1)
    pack[pl.ds(4 * ROWS, nodes, stride=PACK), :] = cut_tail[...].astype(jnp.float32)
    pack[pl.ds(4 * ROWS + 1, nodes, stride=PACK), :] = cut_head[...].astype(jnp.float32)

    for k in (8, 9, 10):
        loads[k].wait()

    def square_one(t, sums):
        costs, wanted = sums
        value = tile(target, t)
        wanted = wanted + value * value
        value = tile(cost_prod, t)
        first = value * value
        value = tile(cost_cut, t)
        other = value * value
        for group in range(groups):
            value = tile(cost_inner, group * tiles + t)
            if group % 2:
                first = first + value * value
            else:
                other = other + value * value
        return costs + (first + other), wanted

    costs, wanted = lax.fori_loop(0, tiles, square_one, (none, none))
    put_summary(send_s, 0, jnp.zeros((tiles, LANES), jnp.float32))
    for row, value in ((0, costs), (2, wanted)):
        value = jnp.sum(value, axis=0, keepdims=True)
        send_s[pl.ds(row, chunks, stride=ROWS), :] = jnp.broadcast_to(value, (chunks, LANES))

    loads[6].wait()
    loads[7].wait()
    tail[...] = tail[...] & (LANES - 1)
    head[...] = head[...] & (LANES - 1)

    def keyed(first, other):
        lane = lax.broadcasted_iota(jnp.int32, first.shape, 1)
        return (first * (LANES * LANES) + other * LANES + lane).astype(jnp.float32)

    keys[pl.ds(0, blocks), :] = keyed(tail[...], head[...])
    keys[pl.ds(blocks, blocks), :] = keyed(head[...], tail[...])
    keys[pl.ds(2 * blocks, nodes), :] = keyed(cut_tail[...], cut_head[...])
    keys[pl.ds(2 * blocks + nodes, nodes), :] = keyed(cut_head[...], cut_tail[...])
    batch = 128

    def sort_batch(k, _):
        at = pl.ds(pl.multiple_of(k * batch, batch), batch)
        ordered = sort_lanes(keys[at, :]).astype(jnp.int32)
        second[at, :] = lax.shift_right_logical(ordered, 7) & (LANES - 1)
        slot[at, :] = ordered & (LANES - 1)
        return 0

    lax.fori_loop(0, (2 * blocks + 2 * nodes) // batch, sort_batch, 0)

    pl.semaphore_wait(pltpu.get_barrier_semaphore(), periods + nodes - 2 + far_count)
    spread_owners(send_a, recv_a, ROWS, 0)
    spread_owners(send_s, recv_s, ROWS, 1)
    spread_nodes(pack, packs, PACK, SENT, 2)

    loads[11].wait()
    loads[12].wait()

    def reorder(step, _):
        moved = []
        for k in range(UNROLL):
            t = step * UNROLL + k
            for group in range(groups):
                j = group * tiles + t
                lanes = lanes_of(slot, j)
                moved.append((flow, j, take(tile(flow, j), lanes)))
                moved.append((cost_inner, j, take(tile(cost_inner, j), lanes)))
            lanes = lanes_of(slot, 2 * blocks + t)
            moved.append((cut, t, take(tile(cut, t), lanes)))
            moved.append((cost_cut, t, take(tile(cost_cut, t), lanes)))
        for ref, number, values in moved:
            put(ref, number, values)
        return 0

    lax.fori_loop(0, tiles // UNROLL, reorder, 0)
    for t in range(ROWS):
        targets[pl.ds(t * tiles, tiles), :] = by_node(target, t)

    await_rows(recv_a, (periods - 1) * ROWS, recv_sem.at[0])
    entering = none
    for j in reversed(range(periods)):
        block = tile(recv_a, j)
        ratio = jnp.where(even, block, pltpu.roll(block, 1, 0))
        put(factor, j, ratio)
        put(give_a, j, entering)
        entering = block + ratio * entering
    give_back(give_a, got_a, ROWS, 3)
    give_far(give_a, far_a, 4)

    await_rows(recv_s, (periods - 1) * ROWS, recv_sem.at[1])
    total = none
    for j in range(periods):
        total = total + tile(recv_s, j)
        factor_c[pl.ds(j * ROWS, ranks), :] = factor[pl.ds(j * ROWS, ranks, stride=2), :]
    part[...] = total
    spread_nodes(part, parts, ROWS, 4, 5, same=True)
    put(parts, me_node, total)

    await_rows(packs, (nodes - 1) * SENT, recv_sem.at[2])
    packs[rows_at(me_node, PACK, PACK), :] = pack[rows_at(me_node, PACK, PACK), :]
    ends_out[...] = take(
        packs[pl.ds(4 * ROWS + 1, nodes, stride=PACK), :], slot[pl.ds(2 * blocks, nodes), :]
    ).astype(jnp.int32)
    ends_in[...] = take(
        packs[pl.ds(4 * ROWS, nodes, stride=PACK), :], slot[pl.ds(2 * blocks + nodes, nodes), :]
    ).astype(jnp.int32)

    def reorder_back(step, _):
        moved = []
        for k in range(UNROLL):
            d = step * UNROLL + k
            lanes = lanes_of(slot, 2 * blocks + nodes + d)
            for place, ref in enumerate((flow_back, cost_back)):
                moved.append((ref, d, take(tile(packs, d * (PACK // ROWS) + place), lanes)))
        for ref, number, values in moved:
            put(ref, number, values)
        return 0

    lax.fori_loop(0, nodes // UNROLL, reorder_back, 0)
    products(lambda t: packs[pl.ds(2 * ROWS + t, nodes, stride=PACK), :], kept_far, grown_far)

    def update_inner(tau):
        def one(step, _):
            stores = []
            for k in range(UNROLL):
                t = step * UNROLL + k
                here = tile(price, t)
                old = tile(prod, t)
                new = jnp.maximum(old - tau * (tile(cost_prod, t) - here), 0.0)
                stores.append((prod, t, new))
                total = 2.0 * new - old
                for group in range(groups):
                    j = group * tiles + t
                    there = take(tile(price, lax.rem(t + group, tiles)), lanes_of(second, j))
                    old = tile(flow, j)
                    new = jnp.maximum(old - tau * (tile(cost_inner, j) - (there - here)), 0.0)
                    moved = 2.0 * new - old
                    stores.append((flow, j, new))
                    stores.append((change, j, moved))
                    total = total - moved
                stores.append((net, t, total))
            for ref, number, values in stores:
                put(ref, number, values)
            return 0

        lax.fori_loop(0, tiles // UNROLL, one, 0)

    def gather_inner():
        def one(step, _):
            stores = []
            for k in range(UNROLL):
                t = step * UNROLL + k
                total = tile(net, t)
                for group in range(groups):
                    j = group * tiles + lax.rem(t - group + tiles, tiles)
                    total = total + take(tile(change, j), lanes_of(second, blocks + j))
                stores.append((net, t, total))
            for ref, number, values in stores:
                put(ref, number, values)
            return 0

        lax.fori_loop(0, tiles // UNROLL, one, 0)

    def update_cut(tau):
        put(price_far, me_node, tile(price, me_node))

        def one(step, _):
            stores = []
            for k in range(UNROLL):
                t = step * UNROLL + k
                here = tile(price, t)
                other = tile(price_far, t)
                there = take(other, lanes_of(ends_out, t))
                old = tile(cut, t)
                new = jnp.maximum(old - tau * (tile(cost_cut, t) - (there - here)), 0.0)
                stores.append((cut, t, new))
                total = tile(net, t) - (2.0 * new - old)
                there = take(other, lanes_of(ends_in, t))
                old = tile(flow_back, t)
                new = jnp.maximum(old - tau * (tile(cost_back, t) - (here - there)), 0.0)
                stores.append((flow_back, t, new))
                stores.append((net, t, total + (2.0 * new - old)))
            for ref, number, values in stores:
                put(ref, number, values)
            return 0

        lax.fori_loop(0, tiles // UNROLL, one, 0)

    await_rows(got_a, (chunks - 1) * ROWS, recv_sem.at[3])
    chain_back(lambda t: at_period(duals, t), kept, get_summary(got_a, 1), price)
    await_rows(parts, (nodes - 1) * 4, recv_sem.at[5])
    sums = [jnp.sum(parts[pl.ds(row, nodes, stride=ROWS), :], keepdims=True) for row in (0, 2)]
    omega = jnp.sqrt(sums[0] / sums[1])
    tau = jnp.broadcast_to(ETA / omega, (ROWS, LANES))
    sigma = ETA * omega
    sigma_tile = jnp.broadcast_to(sigma, (ROWS, LANES)) * (1.0 / horizon)
    sigma_wide = jnp.broadcast_to(sigma, (tiles, LANES))
    sigma_stock = sigma_wide * (1.0 / horizon)
    update_inner(tau)
    gather_inner()
    await_rows(far_a, (nodes - 1) * 2, recv_sem.at[4])
    chain_back(
        lambda t: packs[pl.ds(3 * ROWS + t, nodes, stride=PACK), :], kept_far, by_node(far_a, 1), price_far
    )
    update_cut(tau)

    def local_stock(target_ref):
        stock = None
        for t in range(ROWS):
            value = by_node(net, t)
            stock = value if stock is None else at_period(kept, t) * stock + value
            value = at_period(duals, t) + sigma_wide * (at_period(targets, t) - stock * (1.0 / horizon))
            duals[pl.ds(t * tiles, tiles), :] = value
            if target_ref is not None:
                target_ref[pl.ds(t, tiles, stride=ROWS), :] = value
        return stock

    put_summary(send_b, 0, local_stock(late))
    put_summary(send_b, 1, passed_back())
    spread_owners(send_b, recv_b, ROWS, 6)
    spread_nodes(late, lates, ROWS, ROWS, 7)
    await_rows(recv_b, (periods - 1) * ROWS, recv_sem.at[6])
    entering = none
    entered = []
    for j in range(periods):
        entered.append(entering)
        entering = tile(recv_b, j) + tile(factor, j) * entering
    entering = none
    for j in reversed(range(periods)):
        put(give_b, j, jnp.where(even, entered[j], entering))
        answer = tile(recv_b, j) - sigma_tile * tile(recv_s, j) * pltpu.roll(entered[j], 1, 0)
        entering = answer + tile(factor, j) * entering
    give_back(give_b, got_b, ROWS, 8)
    give_far(give_b, far_b, 9)

    await_rows(got_b, (chunks - 1) * ROWS, recv_sem.at[8])
    stock = get_summary(got_b, 0) * sigma_stock
    for t in range(ROWS):
        duals[pl.ds(t * tiles, tiles), :] = at_period(duals, t) - at_period(grown, t) * stock
    chain_back(lambda t: at_period(duals, t), kept, get_summary(got_b, 1), price)
    update_inner(tau)
    gather_inner()
    await_rows(lates, (nodes - 1) * ROWS, recv_sem.at[7])
    await_rows(far_b, (nodes - 1) * 2, recv_sem.at[9])
    stock_far = by_node(far_b, 0) * sigma_stock
    chain_back(
        lambda t: by_node(lates, t) - at_period(grown_far, t) * stock_far, kept_far, by_node(far_b, 1), price_far
    )
    update_cut(tau)
    put_summary(send_c, 0, local_stock(None), 1)
    spread_owners(send_c, recv_c, ranks, 10)

    def restore(step, _):
        moved = []
        for k in range(UNROLL):
            t = step * UNROLL + k
            for group in range(groups):
                j = group * tiles + t
                moved.append((flow, j, take(tile(flow, j), lanes_of(tail, j))))
            moved.append((cut, t, take(tile(cut, t), lanes_of(cut_tail, t))))
        for ref, number, values in moved:
            put(ref, number, values)
        return 0

    lax.fori_loop(0, tiles // UNROLL, restore, 0)

    await_rows(recv_c, (periods - 1) * ranks, recv_sem.at[10])
    entering = jnp.zeros((ranks, LANES), jnp.float32)
    for j in range(periods):
        give_c[pl.ds(j * ROWS, ranks), :] = entering
        entering = recv_c[pl.ds(j * ROWS, ranks), :] + factor_c[pl.ds(j * ROWS, ranks), :] * entering
    give_back(give_c, got_c, ranks, 11)
    await_rows(got_c, (chunks - 1) * ranks, recv_sem.at[11])
    stock = get_summary(got_c, 0, 1) * sigma_stock
    for t in range(ROWS):
        dual[pl.ds(t, tiles, stride=ROWS), :] = at_period(duals, t) - at_period(grown, t) * stock

    for phase, rows in (
        (0, (periods - 1) * ROWS),
        (1, (periods - 1) * ROWS),
        (2, (nodes - 1) * SENT),
        (3, (chunks - 1) * ROWS),
        (5, (nodes - 1) * 4),
        (6, (periods - 1) * ROWS),
        (7, (nodes - 1) * ROWS),
        (8, (chunks - 1) * ROWS),
        (10, (periods - 1) * ranks),
        (11, (chunks - 1) * ranks),
    ):
        await_rows(packs, rows, send_sem.at[phase])
    for phase in (4, 9):
        await_rows(packs, chunks * (ranks - 1) * 2, send_sem.at[phase])

        @pl.when(me_chunk != node_chunk)
        def _():
            await_rows(packs, chunks * 2, send_sem.at[phase])


def hand_over(count, *refs):
    semaphores = refs[-1]
    copies = [
        pltpu.make_async_copy(refs[k], refs[count + k], semaphores.at[k]) for k in range(count)
    ]
    for copy in copies:
        copy.start()
    for copy in copies:
        copy.wait()


def solution(mesh):
    nodes, periods = mesh.shape["node"], mesh.shape["period"]

    def to_tiles(values):
        rows, columns = values.shape
        return values.reshape(rows, columns // LANES, LANES).transpose(1, 0, 2).reshape(-1, LANES)

    def from_tiles(values):
        count = values.shape[0] // ROWS
        return values.reshape(count, ROWS, LANES).transpose(1, 0, 2).reshape(ROWS, count * LANES)

    def body(*operands):
        floats = [to_tiles(values) for values in operands[:9]]
        indices = [values.reshape(-1, LANES) for values in operands[9:]]
        tiles = floats[0].shape[0] // ROWS
        groups = floats[1].shape[0] // floats[0].shape[0]
        blocks = tiles * groups
        slab = (tiles * ROWS, LANES)
        arcs = (blocks * ROWS, LANES)
        ring = (periods * ROWS, LANES)
        sorts = (2 * blocks + 2 * nodes, LANES)

        def room(shape, kind=jnp.float32):
            return pltpu.VMEM(shape, kind)

        scratch = [
            room(slab), room(arcs), room(slab), room(slab), room(slab),
            room((blocks, LANES), jnp.int32), room((blocks, LANES), jnp.int32),
            room((tiles, LANES), jnp.int32), room((tiles, LANES), jnp.int32),
            room(slab), room(slab), room(slab), room(slab), room(slab), room(slab),
            room(slab), room(slab), room(slab), room(arcs),
            room(sorts), room(sorts, jnp.int32), room(sorts, jnp.int32),
            room((nodes, LANES), jnp.int32), room((nodes, LANES), jnp.int32),
            room((nodes * PACK, LANES)), room((nodes * PACK, LANES)), room(slab), room(slab),
            room(slab), room(slab), room((ROWS, LANES)), room(slab),
            room(ring), room(ring), room(ring), room(ring), room(slab), room(ring), room(ring),
            room(ring), room(ring), room(ring), room(ring), room(slab),
            room(ring), room(ring), room(ring), room(ring),
            room(ring), room(ring),
            pltpu.SemaphoreType.DMA((13,)),
            pltpu.SemaphoreType.DMA((12,)),
            pltpu.SemaphoreType.DMA((12,)),
        ]
        anywhere = pl.BlockSpec(memory_space=pl.ANY)
        inside = pl.BlockSpec(memory_space=pltpu.VMEM)
        shapes = (slab, arcs, slab, slab)
        results = pl.pallas_call(
            functools.partial(kernel, (nodes, periods, tiles, groups)),
            out_shape=[pltpu.VMEM(shape, jnp.float32) for shape in shapes],
            in_specs=[anywhere] * 13,
            out_specs=[inside] * 4,
            scratch_shapes=scratch,
            compiler_params=pltpu.CompilerParams(
                collective_id=0, has_side_effects=True, vmem_limit_bytes=LIMIT
            ),
        )(*floats, *indices)
        outputs = pl.pallas_call(
            functools.partial(hand_over, 4),
            out_shape=[jax.ShapeDtypeStruct(shape, jnp.float32) for shape in shapes],
            in_specs=[anywhere] * 4,
            out_specs=[anywhere] * 4,
            scratch_shapes=[pltpu.SemaphoreType.DMA((4,))],
            compiler_params=pltpu.CompilerParams(vmem_limit_bytes=LIMIT // 8),
        )(*results)
        return tuple(from_tiles(values) for values in outputs)

    both, node = P("period", "node"), P("node")
    return jax.shard_map(
        body,
        mesh=mesh,
        in_specs=(both,) * 9 + (node,) * 4,
        out_specs=(both,) * 4,
        check_vma=False,
    )
```

```python
import functools

import jax
import jax.numpy as jnp
from jax import lax
from jax.experimental import pallas as pl
from jax.experimental.pallas import tpu as pltpu
from jax.sharding import PartitionSpec as P

MESH = pl.DeviceIdType.MESH
ETA = 0.25
LANES = 128
ROWS = 8
PACK = 40
SENT = 34
UNROLL = 16
LIMIT = 56 * 1024 * 1024


def take(values, lanes):
    return jnp.take_along_axis(values, lanes, axis=1, mode="promise_in_bounds")


def sort_lanes(values):
    lane = lax.broadcasted_iota(jnp.int32, values.shape, 1)
    size = 2
    while size <= LANES:
        step = size // 2
        while step:
            other = take(values, lane ^ step)
            low = ((lane & size) == 0) == ((lane & step) == 0)
            values = jnp.where(low, jnp.minimum(values, other), jnp.maximum(values, other))
            step //= 2
        size *= 2
    return values


def kernel(sizes, *refs):
    nodes, periods, tiles, groups = sizes
    (
        prod_in, flow_in, cut_in, dual_in, cost_prod_in, cost_inner_in, cost_cut_in, target_in, keep_in,
        tail_in, head_in, cut_tail_in, cut_head_in,
        prod, flow, cut, dual,
        cost_prod, cost_inner, cost_cut, target, keep,
        tail, head, cut_tail, cut_head,
        kept, duals, targets, grown, kept_far, grown_far,
        price, price_far, net, change,
        keys, second, slot, ends_out, ends_in,
        pack, packs, flow_back, cost_back,
        late, lates, part, parts, whole, wholes,
        send_a, recv_a, give_a, got_a, far_a, send_s, recv_s,
        send_b, recv_b, give_b, got_b, far_b,
        send_c, recv_c, give_c, got_c,
        factor, factor_c,
        in_sem, send_sem, recv_sem,
    ) = refs
    me_node = lax.axis_index("node")
    me_period = lax.axis_index("period")
    horizon = periods * ROWS
    blocks = groups * tiles
    chunks = periods // 2
    reach = chunks // 2
    ranks = tiles // chunks
    me_chunk = lax.rem(me_period, chunks)

    def rows_at(number, rows=ROWS, pitch=ROWS):
        return pl.ds(pl.multiple_of(number * pitch, ROWS), rows)

    def tile(ref, number):
        return ref[rows_at(number), :]

    def put(ref, number, values):
        ref[rows_at(number), :] = values

    def lanes_of(ref, number):
        return jnp.broadcast_to(ref[pl.ds(number, 1), :], (ROWS, LANES))

    loads = [
        pltpu.make_async_copy(source, target_ref, in_sem.at[k])
        for k, (source, target_ref) in enumerate(
            (
                (keep_in, keep),
                (dual_in, dual),
                (cut_tail_in, cut_tail),
                (cut_head_in, cut_head),
                (cut_in, cut),
                (cost_cut_in, cost_cut),
                (tail_in, tail),
                (head_in, head),
                (target_in, target),
                (cost_prod_in, cost_prod),
                (cost_inner_in, cost_inner),
                (flow_in, flow),
                (prod_in, prod),
            )
        )
    ]
    def greet(device):
        pl.semaphore_signal(
            pltpu.get_barrier_semaphore(), inc=1, device_id=device, device_id_type=MESH
        )

    def around(i):
        return lax.rem(
            me_period + periods // 2 + (1 - 2 * lax.rem(i, 2)) * lax.div(i + 1, 2), periods
        )

    def away(i):
        return lax.rem(2 + i + lax.div(i, 2) + 2 * lax.div(i, 3), 4)

    def across(k):
        y = lax.rem(lax.div(me_node, 8) + away(lax.div(k, 8)), 4)
        x = lax.rem(lax.div(me_node, 2) + away(lax.rem(lax.div(k, 2), 4)), 4)
        return y * 8 + x * 2 + lax.rem(me_node + 1 + k, 2)

    def greet_period(k, _):
        greet({"period": around(k)})
        return 0

    def greet_node(k, _):
        greet({"node": across(k)})
        return 0

    node_chunk = lax.rem(me_node, chunks)
    source_plane = node_chunk + chunks * (
        lax.rem(me_period + periods + reach - node_chunk, periods) // chunks
    )

    def greet_far(k, _):
        greet({"node": across(k), "period": source_plane})
        return 0

    for load in loads[:2]:
        load.start()
    lax.fori_loop(0, periods - 1, greet_period, 0)
    for load in loads[2:]:
        load.start()
    lax.fori_loop(0, nodes - 1, greet_far, 0)
    lax.fori_loop(0, nodes - 1, greet_node, 0)
    far_count = jnp.where(me_chunk == node_chunk, ranks - 1, ranks) * chunks

    def start(source, target_ref, source_rows, target_rows, phase, device):
        pltpu.make_async_remote_copy(
            src_ref=source.at[source_rows, :],
            dst_ref=target_ref.at[target_rows, :],
            send_sem=send_sem.at[phase],
            recv_sem=recv_sem.at[phase],
            device_id=device,
            device_id_type=MESH,
        ).start()

    def spread_owners(source, target_ref, rows, phase):
        def one(k, _):
            peer = around(k)
            start(
                source, target_ref, rows_at(lax.rem(peer, chunks), rows), rows_at(me_period, rows), phase,
                {"period": peer},
            )
            return 0

        lax.fori_loop(0, periods - 1, one, 0)
        put(target_ref, me_period, tile(source, me_chunk))

    def served(i):
        return lax.rem(
            me_period + periods - reach + lax.div(i, 2) + lax.rem(i, 2) * (chunks - 1 - 2 * lax.div(i, 2)), periods
        )

    def give(source, rows, own_ref, phase, far_ref=None, far_phase=None):
        def one(i, _):
            peer = served(i)
            if far_ref is not None:
                for rank in range(ranks):
                    to = me_chunk + rank * chunks

                    @pl.when(to != me_node)
                    def _():
                        start(
                            source, far_ref,
                            pl.ds(pl.multiple_of(peer * ROWS, ROWS) + 2 * rank, 2), rows_at(me_node, 2), far_phase,
                            {"node": to, "period": peer},
                        )

            @pl.when(peer != me_period)
            def _():
                start(
                    source, own_ref, rows_at(peer, rows), rows_at(me_chunk, rows), phase, {"period": peer}
                )

            return 0

        lax.fori_loop(0, chunks, one, 0)
        put(own_ref, me_chunk, tile(source, me_period))

    def spread_nodes(source, target_ref, pitch, rows, phase, same=False):
        def one(k, _):
            peer = across(k)
            start(
                source, target_ref, rows_at(0 if same else peer, rows, pitch), rows_at(me_node, rows, pitch), phase,
                {"node": peer},
            )
            return 0

        lax.fori_loop(0, nodes - 1, one, 0)

    def await_rows(ref, rows, semaphore):
        span = ref.at[pl.ds(0, rows), :]
        pltpu.make_async_copy(span, span, semaphore).wait()

    def put_summary(ref, row, values, pitch=2):
        for rank in range(ranks):
            ref[pl.ds(pitch * rank + row, chunks, stride=ROWS), :] = values[
                rank * chunks : (rank + 1) * chunks
            ]

    def get_summary(ref, row, pitch=2):
        return jnp.concatenate(
            [ref[pl.ds(pitch * rank + row, chunks, stride=ROWS), :] for rank in range(ranks)], axis=0
        )

    def at_period(ref, t):
        return ref[pl.ds(t * tiles, tiles), :]

    def by_node(ref, t, pitch=ROWS):
        return ref[pl.ds(t, tiles, stride=pitch), :]

    def chain_back(values, shares, entering, target_ref):
        for t in reversed(range(ROWS)):
            entering = values(t) + entering
            target_ref[pl.ds(t, tiles, stride=ROWS), :] = entering * (1.0 / horizon)
            entering = entering * at_period(shares, t)

    def passed_back():
        passed = None
        for t in reversed(range(ROWS)):
            value = at_period(duals, t)
            passed = value if passed is None else value + passed
            passed = passed * at_period(kept, t)
        return passed

    def products(share_of, shares, target_ref):
        product = None
        square_sum = None
        for t in range(ROWS):
            share = share_of(t)
            shares[pl.ds(t * tiles, tiles), :] = share
            product = share if product is None else product * share
            target_ref[pl.ds(t * tiles, tiles), :] = product
            square = product * product
            square_sum = square if square_sum is None else square_sum + square
        return product, square_sum

    even = (lax.broadcasted_iota(jnp.int32, (ROWS, LANES), 0) & 1) == 0
    none = jnp.zeros((ROWS, LANES), jnp.float32)

    loads[0].wait()
    loads[1].wait()
    product, square_sum = products(lambda t: by_node(keep, t), kept, grown)
    for t in range(ROWS):
        duals[pl.ds(t * tiles, tiles), :] = by_node(dual, t)
    put_summary(send_a, 0, product)
    put_summary(send_a, 1, passed_back())
    put_summary(send_s, 1, square_sum)

    for k in (2, 3, 4, 5):
        loads[k].wait()

    def pack_one(step, _):
        for k in range(UNROLL):
            d = step * UNROLL + k
            for place, ref in enumerate((cut, cost_cut, keep, dual)):
                pack[rows_at(d * (PACK // ROWS) + place), :] = tile(ref, d)
        return 0

    lax.fori_loop(0, nodes // UNROLL, pack_one, 0)
    cut_tail[...] = cut_tail[...] & (LANES - 1)
    cut_head[...] = cut_head[...] & (LANES - 1)
    pack[pl.ds(4 * ROWS, nodes, stride=PACK), :] = cut_tail[...].astype(jnp.float32)
    pack[pl.ds(4 * ROWS + 1, nodes, stride=PACK), :] = cut_head[...].astype(jnp.float32)

    for k in (8, 9, 10):
        loads[k].wait()

    def square_one(t, sums):
        costs, wanted = sums
        value = tile(target, t)
        wanted = wanted + value * value
        value = tile(cost_prod, t)
        first = value * value
        value = tile(cost_cut, t)
        other = value * value
        for group in range(groups):
            value = tile(cost_inner, group * tiles + t)
            if group % 2:
                first = first + value * value
            else:
                other = other + value * value
        return costs + (first + other), wanted

    costs, wanted = lax.fori_loop(0, tiles, square_one, (none, none))
    first_row = lax.broadcasted_iota(jnp.int32, (ROWS, LANES), 0) < 1
    part[...] = jnp.where(
        first_row, jnp.sum(costs, axis=0, keepdims=True), jnp.sum(wanted, axis=0, keepdims=True)
    )

    pl.semaphore_wait(pltpu.get_barrier_semaphore(), periods + nodes - 2 + far_count)
    spread_owners(send_a, recv_a, ROWS, 0)
    spread_nodes(part, parts, ROWS, 2, 5, same=True)
    put(parts, me_node, part[...])
    spread_owners(send_s, recv_s, ROWS, 1)
    spread_nodes(pack, packs, PACK, SENT, 2)

    loads[6].wait()
    loads[7].wait()
    tail[...] = tail[...] & (LANES - 1)
    head[...] = head[...] & (LANES - 1)

    def keyed(first, other):
        lane = lax.broadcasted_iota(jnp.int32, first.shape, 1)
        return (first * (LANES * LANES) + other * LANES + lane).astype(jnp.float32)

    keys[pl.ds(0, blocks), :] = keyed(tail[...], head[...])
    keys[pl.ds(blocks, blocks), :] = keyed(head[...], tail[...])
    keys[pl.ds(2 * blocks, nodes), :] = keyed(cut_tail[...], cut_head[...])
    keys[pl.ds(2 * blocks + nodes, nodes), :] = keyed(cut_head[...], cut_tail[...])
    batch = 2 * blocks + 2 * nodes

    def sort_batch(k, _):
        at = pl.ds(pl.multiple_of(k * batch, batch), batch)
        ordered = sort_lanes(keys[at, :]).astype(jnp.int32)
        second[at, :] = lax.shift_right_logical(ordered, 7) & (LANES - 1)
        slot[at, :] = ordered & (LANES - 1)
        return 0

    lax.fori_loop(0, (2 * blocks + 2 * nodes) // batch, sort_batch, 0)

    loads[11].wait()
    loads[12].wait()

    def reorder(step, _):
        moved = []
        for k in range(UNROLL):
            t = step * UNROLL + k
            for group in range(groups):
                j = group * tiles + t
                lanes = lanes_of(slot, j)
                moved.append((flow, j, take(tile(flow, j), lanes)))
                moved.append((cost_inner, j, take(tile(cost_inner, j), lanes)))
            lanes = lanes_of(slot, 2 * blocks + t)
            moved.append((cut, t, take(tile(cut, t), lanes)))
            moved.append((cost_cut, t, take(tile(cost_cut, t), lanes)))
        for ref, number, values in moved:
            put(ref, number, values)
        return 0

    lax.fori_loop(0, tiles // UNROLL, reorder, 0)
    for t in range(ROWS):
        targets[pl.ds(t * tiles, tiles), :] = by_node(target, t)

    await_rows(parts, (nodes - 1) * 2, recv_sem.at[5])
    whole[...] = jnp.where(
        first_row,
        jnp.sum(parts[pl.ds(0, nodes, stride=ROWS), :], axis=0, keepdims=True),
        jnp.sum(parts[pl.ds(1, nodes, stride=ROWS), :], axis=0, keepdims=True),
    )

    def spread_whole(k, _):
        start(whole, wholes, rows_at(0, 2), rows_at(me_period, 2), 12, {"period": around(k)})
        return 0

    lax.fori_loop(0, periods - 1, spread_whole, 0)
    put(wholes, me_period, whole[...])

    await_rows(recv_a, (periods - 1) * ROWS, recv_sem.at[0])
    entering = none
    for j in reversed(range(periods)):
        block = tile(recv_a, j)
        ratio = jnp.where(even, block, pltpu.roll(block, 1, 0))
        put(factor, j, ratio)
        put(give_a, j, entering)
        entering = block + ratio * entering
    give(give_a, ROWS, got_a, 3, far_a, 4)

    await_rows(recv_s, (periods - 1) * ROWS, recv_sem.at[1])
    for j in range(periods):
        factor_c[pl.ds(j * ROWS, ranks), :] = factor[pl.ds(j * ROWS, ranks, stride=2), :]

    await_rows(packs, (nodes - 1) * SENT, recv_sem.at[2])
    packs[rows_at(me_node, PACK, PACK), :] = pack[rows_at(me_node, PACK, PACK), :]
    ends_out[...] = take(
        packs[pl.ds(4 * ROWS + 1, nodes, stride=PACK), :], slot[pl.ds(2 * blocks, nodes), :]
    ).astype(jnp.int32)
    ends_in[...] = take(
        packs[pl.ds(4 * ROWS, nodes, stride=PACK), :], slot[pl.ds(2 * blocks + nodes, nodes), :]
    ).astype(jnp.int32)

    def reorder_back(step, _):
        moved = []
        for k in range(UNROLL):
            d = step * UNROLL + k
            lanes = lanes_of(slot, 2 * blocks + nodes + d)
            for place, ref in enumerate((flow_back, cost_back)):
                moved.append((ref, d, take(tile(packs, d * (PACK // ROWS) + place), lanes)))
        for ref, number, values in moved:
            put(ref, number, values)
        return 0

    lax.fori_loop(0, nodes // UNROLL, reorder_back, 0)
    products(lambda t: packs[pl.ds(2 * ROWS + t, nodes, stride=PACK), :], kept_far, grown_far)

    def update_inner(tau):
        def one(step, _):
            stores = []
            for k in range(UNROLL):
                t = step * UNROLL + k
                here = tile(price, t)
                old = tile(prod, t)
                new = jnp.maximum(old - tau * (tile(cost_prod, t) - here), 0.0)
                stores.append((prod, t, new))
                total = 2.0 * new - old
                for group in range(groups):
                    j = group * tiles + t
                    there = take(tile(price, lax.rem(t + group, tiles)), lanes_of(second, j))
                    old = tile(flow, j)
                    new = jnp.maximum(old - tau * (tile(cost_inner, j) - (there - here)), 0.0)
                    moved = 2.0 * new - old
                    stores.append((flow, j, new))
                    stores.append((change, j, moved))
                    total = total - moved
                stores.append((net, t, total))
            for ref, number, values in stores:
                put(ref, number, values)
            return 0

        lax.fori_loop(0, tiles // UNROLL, one, 0)

    def gather_inner():
        def one(step, _):
            stores = []
            for k in range(UNROLL):
                t = step * UNROLL + k
                total = tile(net, t)
                for group in range(groups):
                    j = group * tiles + lax.rem(t - group + tiles, tiles)
                    total = total + take(tile(change, j), lanes_of(second, blocks + j))
                stores.append((net, t, total))
            for ref, number, values in stores:
                put(ref, number, values)
            return 0

        lax.fori_loop(0, tiles // UNROLL, one, 0)

    def update_cut(tau):
        put(price_far, me_node, tile(price, me_node))

        def one(step, _):
            stores = []
            for k in range(UNROLL):
                t = step * UNROLL + k
                here = tile(price, t)
                other = tile(price_far, t)
                there = take(other, lanes_of(ends_out, t))
                old = tile(cut, t)
                new = jnp.maximum(old - tau * (tile(cost_cut, t) - (there - here)), 0.0)
                stores.append((cut, t, new))
                total = tile(net, t) - (2.0 * new - old)
                there = take(other, lanes_of(ends_in, t))
                old = tile(flow_back, t)
                new = jnp.maximum(old - tau * (tile(cost_back, t) - (here - there)), 0.0)
                stores.append((flow_back, t, new))
                stores.append((net, t, total + (2.0 * new - old)))
            for ref, number, values in stores:
                put(ref, number, values)
            return 0

        lax.fori_loop(0, tiles // UNROLL, one, 0)

    await_rows(got_a, (chunks - 1) * ROWS, recv_sem.at[3])
    chain_back(lambda t: at_period(duals, t), kept, get_summary(got_a, 1), price)
    await_rows(wholes, (periods - 1) * 2, recv_sem.at[12])
    sums = [jnp.sum(wholes[pl.ds(row, periods, stride=ROWS), :], keepdims=True) for row in range(2)]
    omega = jnp.sqrt(sums[0] / sums[1])
    tau = jnp.broadcast_to(ETA / omega, (ROWS, LANES))
    sigma = ETA * omega
    sigma_tile = jnp.broadcast_to(sigma, (ROWS, LANES)) * (1.0 / horizon)
    sigma_wide = jnp.broadcast_to(sigma, (tiles, LANES))
    sigma_stock = sigma_wide * (1.0 / horizon)
    update_inner(tau)
    gather_inner()
    await_rows(far_a, (nodes - 1) * 2, recv_sem.at[4])
    chain_back(
        lambda t: packs[pl.ds(3 * ROWS + t, nodes, stride=PACK), :], kept_far, by_node(far_a, 1), price_far
    )
    update_cut(tau)

    def local_stock(target_ref):
        stock = None
        for t in range(ROWS):
            value = by_node(net, t)
            stock = value if stock is None else at_period(kept, t) * stock + value
            value = at_period(duals, t) + sigma_wide * (at_period(targets, t) - stock * (1.0 / horizon))
            duals[pl.ds(t * tiles, tiles), :] = value
            if target_ref is not None:
                target_ref[pl.ds(t, tiles, stride=ROWS), :] = value
        return stock

    put_summary(send_b, 0, local_stock(late))
    put_summary(send_b, 1, passed_back())
    spread_owners(send_b, recv_b, ROWS, 6)
    spread_nodes(late, lates, ROWS, ROWS, 7)
    await_rows(recv_b, (periods - 1) * ROWS, recv_sem.at[6])
    entering = none
    entered = []
    for j in range(periods):
        entered.append(entering)
        entering = tile(recv_b, j) + tile(factor, j) * entering
    entering = none
    for j in reversed(range(periods)):
        put(give_b, j, jnp.where(even, entered[j], entering))
        answer = tile(recv_b, j) - sigma_tile * tile(recv_s, j) * pltpu.roll(entered[j], 1, 0)
        entering = answer + tile(factor, j) * entering
    give(give_b, ROWS, got_b, 8, far_b, 9)

    await_rows(got_b, (chunks - 1) * ROWS, recv_sem.at[8])
    stock = get_summary(got_b, 0) * sigma_stock
    for t in range(ROWS):
        duals[pl.ds(t * tiles, tiles), :] = at_period(duals, t) - at_period(grown, t) * stock
    chain_back(lambda t: at_period(duals, t), kept, get_summary(got_b, 1), price)
    update_inner(tau)
    gather_inner()
    await_rows(lates, (nodes - 1) * ROWS, recv_sem.at[7])
    await_rows(far_b, (nodes - 1) * 2, recv_sem.at[9])
    stock_far = by_node(far_b, 0) * sigma_stock
    chain_back(
        lambda t: by_node(lates, t) - at_period(grown_far, t) * stock_far, kept_far, by_node(far_b, 1), price_far
    )
    update_cut(tau)
    put_summary(send_c, 0, local_stock(None), 1)
    spread_owners(send_c, recv_c, ranks, 10)

    def restore(step, _):
        moved = []
        for k in range(UNROLL):
            t = step * UNROLL + k
            for group in range(groups):
                j = group * tiles + t
                moved.append((flow, j, take(tile(flow, j), lanes_of(tail, j))))
            moved.append((cut, t, take(tile(cut, t), lanes_of(cut_tail, t))))
        for ref, number, values in moved:
            put(ref, number, values)
        return 0

    lax.fori_loop(0, tiles // UNROLL, restore, 0)

    await_rows(recv_c, (periods - 1) * ranks, recv_sem.at[10])
    entering = jnp.zeros((ranks, LANES), jnp.float32)
    for j in range(periods):
        give_c[pl.ds(j * ROWS, ranks), :] = entering
        entering = recv_c[pl.ds(j * ROWS, ranks), :] + factor_c[pl.ds(j * ROWS, ranks), :] * entering
    give(give_c, ranks, got_c, 11)
    await_rows(got_c, (chunks - 1) * ranks, recv_sem.at[11])
    stock = get_summary(got_c, 0, 1) * sigma_stock
    for t in range(ROWS):
        dual[pl.ds(t, tiles, stride=ROWS), :] = at_period(duals, t) - at_period(grown, t) * stock

    for phase, rows in (
        (0, (periods - 1) * ROWS),
        (1, (periods - 1) * ROWS),
        (2, (nodes - 1) * SENT),
        (3, (chunks - 1) * ROWS),
        (5, (nodes - 1) * 2),
        (12, (periods - 1) * 2),
        (6, (periods - 1) * ROWS),
        (7, (nodes - 1) * ROWS),
        (8, (chunks - 1) * ROWS),
        (10, (periods - 1) * ranks),
        (11, (chunks - 1) * ranks),
    ):
        await_rows(packs, rows, send_sem.at[phase])
    for phase in (4, 9):
        await_rows(packs, chunks * (ranks - 1) * 2, send_sem.at[phase])

        @pl.when(me_chunk != node_chunk)
        def _():
            await_rows(packs, chunks * 2, send_sem.at[phase])


def hand_over(count, *refs):
    semaphores = refs[-1]
    copies = [
        pltpu.make_async_copy(refs[k], refs[count + k], semaphores.at[k]) for k in range(count)
    ]
    for copy in copies:
        copy.start()
    for copy in copies:
        copy.wait()


def solution(mesh):
    nodes, periods = mesh.shape["node"], mesh.shape["period"]

    def to_tiles(values):
        rows, columns = values.shape
        return values.reshape(rows, columns // LANES, LANES).transpose(1, 0, 2).reshape(-1, LANES)

    def from_tiles(values):
        count = values.shape[0] // ROWS
        return values.reshape(count, ROWS, LANES).transpose(1, 0, 2).reshape(ROWS, count * LANES)

    def body(*operands):
        floats = [to_tiles(values) for values in operands[:9]]
        indices = [values.reshape(-1, LANES) for values in operands[9:]]
        tiles = floats[0].shape[0] // ROWS
        groups = floats[1].shape[0] // floats[0].shape[0]
        blocks = tiles * groups
        slab = (tiles * ROWS, LANES)
        arcs = (blocks * ROWS, LANES)
        ring = (periods * ROWS, LANES)
        sorts = (2 * blocks + 2 * nodes, LANES)

        def room(shape, kind=jnp.float32):
            return pltpu.VMEM(shape, kind)

        scratch = [
            room(slab), room(arcs), room(slab), room(slab), room(slab),
            room((blocks, LANES), jnp.int32), room((blocks, LANES), jnp.int32),
            room((tiles, LANES), jnp.int32), room((tiles, LANES), jnp.int32),
            room(slab), room(slab), room(slab), room(slab), room(slab), room(slab),
            room(slab), room(slab), room(slab), room(arcs),
            room(sorts), room(sorts, jnp.int32), room(sorts, jnp.int32),
            room((nodes, LANES), jnp.int32), room((nodes, LANES), jnp.int32),
            room((nodes * PACK, LANES)), room((nodes * PACK, LANES)), room(slab), room(slab),
            room(slab), room(slab), room((ROWS, LANES)), room(slab), room((ROWS, LANES)), room(ring),
            room(ring), room(ring), room(ring), room(ring), room(slab), room(ring), room(ring),
            room(ring), room(ring), room(ring), room(ring), room(slab),
            room(ring), room(ring), room(ring), room(ring),
            room(ring), room(ring),
            pltpu.SemaphoreType.DMA((13,)),
            pltpu.SemaphoreType.DMA((13,)),
            pltpu.SemaphoreType.DMA((13,)),
        ]
        anywhere = pl.BlockSpec(memory_space=pl.ANY)
        inside = pl.BlockSpec(memory_space=pltpu.VMEM)
        shapes = (slab, arcs, slab, slab)
        results = pl.pallas_call(
            functools.partial(kernel, (nodes, periods, tiles, groups)),
            out_shape=[pltpu.VMEM(shape, jnp.float32) for shape in shapes],
            in_specs=[anywhere] * 13,
            out_specs=[inside] * 4,
            scratch_shapes=scratch,
            compiler_params=pltpu.CompilerParams(
                collective_id=0, has_side_effects=True, vmem_limit_bytes=LIMIT
            ),
        )(*floats, *indices)
        outputs = pl.pallas_call(
            functools.partial(hand_over, 4),
            out_shape=[jax.ShapeDtypeStruct(shape, jnp.float32) for shape in shapes],
            in_specs=[anywhere] * 4,
            out_specs=[anywhere] * 4,
            scratch_shapes=[pltpu.SemaphoreType.DMA((4,))],
            compiler_params=pltpu.CompilerParams(vmem_limit_bytes=LIMIT // 8),
        )(*results)
        return tuple(from_tiles(values) for values in outputs)

    both, node = P("period", "node"), P("node")
    return jax.shard_map(
        body,
        mesh=mesh,
        in_specs=(both,) * 9 + (node,) * 4,
        out_specs=(both,) * 4,
        check_vma=False,
    )
```

```python
import functools

import jax
import jax.numpy as jnp
from jax import lax
from jax.experimental import pallas as pl
from jax.experimental.pallas import tpu as pltpu
from jax.sharding import PartitionSpec as P

MESH = pl.DeviceIdType.MESH
ETA = 0.25
LANES = 128
ROWS = 8
PACK = 40
SENT = 34
UNROLL = 16
LIMIT = 56 * 1024 * 1024


def take(values, lanes):
    return jnp.take_along_axis(values, lanes, axis=1, mode="promise_in_bounds")


def sort_lanes(values):
    lane = lax.broadcasted_iota(jnp.int32, values.shape, 1)
    size = 2
    while size <= LANES:
        step = size // 2
        while step:
            other = take(values, lane ^ step)
            low = ((lane & size) == 0) == ((lane & step) == 0)
            values = jnp.where(low, jnp.minimum(values, other), jnp.maximum(values, other))
            step //= 2
        size *= 2
    return values


def kernel(sizes, *refs):
    nodes, periods, tiles, groups = sizes
    (
        prod_in, flow_in, cut_in, dual_in, cost_prod_in, cost_inner_in, cost_cut_in, target_in, keep_in,
        tail_in, head_in, cut_tail_in, cut_head_in,
        prod, flow, cut, dual,
        cost_prod, cost_inner, cost_cut, target, keep,
        tail, head, cut_tail, cut_head,
        kept, duals, targets, grown, kept_far, grown_far,
        price, price_far, net, change,
        keys, second, slot, ends_out, ends_in,
        pack, packs, flow_back, cost_back,
        late, lates, part, parts, whole, wholes,
        send_a, recv_a, give_a, got_a, far_a, send_s, recv_s,
        send_b, recv_b, give_b, got_b, far_b,
        send_c, recv_c, give_c, got_c,
        factor, factor_c,
        in_sem, send_sem, recv_sem,
    ) = refs
    me_node = lax.axis_index("node")
    me_period = lax.axis_index("period")
    horizon = periods * ROWS
    blocks = groups * tiles
    chunks = periods // 2
    reach = chunks // 2
    ranks = tiles // chunks
    me_chunk = lax.rem(me_period, chunks)

    def rows_at(number, rows=ROWS, pitch=ROWS):
        return pl.ds(pl.multiple_of(number * pitch, ROWS), rows)

    def tile(ref, number):
        return ref[rows_at(number), :]

    def put(ref, number, values):
        ref[rows_at(number), :] = values

    def lanes_of(ref, number):
        return jnp.broadcast_to(ref[pl.ds(number, 1), :], (ROWS, LANES))

    loads = [
        pltpu.make_async_copy(source, target_ref, in_sem.at[k])
        for k, (source, target_ref) in enumerate(
            (
                (keep_in, keep),
                (dual_in, dual),
                (cut_tail_in, cut_tail),
                (cut_head_in, cut_head),
                (cut_in, cut),
                (cost_cut_in, cost_cut),
                (tail_in, tail),
                (head_in, head),
                (target_in, target),
                (cost_prod_in, cost_prod),
                (cost_inner_in, cost_inner),
                (flow_in, flow),
                (prod_in, prod),
            )
        )
    ]
    def greet(device):
        pl.semaphore_signal(
            pltpu.get_barrier_semaphore(), inc=1, device_id=device, device_id_type=MESH
        )

    def around(i):
        return lax.rem(
            me_period + periods // 2 + (1 - 2 * lax.rem(i, 2)) * lax.div(i + 1, 2), periods
        )

    def away(i):
        return lax.rem(2 + i + lax.div(i, 2) + 2 * lax.div(i, 3), 4)

    def across(k):
        y = lax.rem(lax.div(me_node, 8) + away(lax.div(k, 8)), 4)
        x = lax.rem(lax.div(me_node, 2) + away(lax.rem(lax.div(k, 2), 4)), 4)
        return y * 8 + x * 2 + lax.rem(me_node + 1 + k, 2)

    def greet_period(k, _):
        greet({"period": around(k)})
        return 0

    def greet_node(k, _):
        greet({"node": across(k)})
        return 0

    node_chunk = lax.rem(me_node, chunks)

    for load in loads[:2]:
        load.start()
    lax.fori_loop(0, periods - 1, greet_period, 0)
    for load in loads[2:]:
        load.start()
    lax.fori_loop(0, nodes - 1, greet_node, 0)

    def start(source, target_ref, source_rows, target_rows, phase, device):
        pltpu.make_async_remote_copy(
            src_ref=source.at[source_rows, :],
            dst_ref=target_ref.at[target_rows, :],
            send_sem=send_sem.at[phase],
            recv_sem=recv_sem.at[phase],
            device_id=device,
            device_id_type=MESH,
        ).start()

    def spread_owners(source, target_ref, rows, phase):
        def one(k, _):
            peer = around(k)
            start(
                source, target_ref, rows_at(lax.rem(peer, chunks), rows), rows_at(me_period, rows), phase,
                {"period": peer},
            )
            return 0

        lax.fori_loop(0, periods - 1, one, 0)
        put(target_ref, me_period, tile(source, me_chunk))

    def served(i):
        return lax.rem(
            me_period + periods - reach + lax.div(i, 2) + lax.rem(i, 2) * (chunks - 1 - 2 * lax.div(i, 2)), periods
        )

    def give(source, rows, own_ref, phase, far_ref=None, far_phase=None):
        def one(i, _):
            peer = served(i)
            if far_ref is not None:
                for rank in range(ranks):
                    to = me_chunk + rank * chunks

                    @pl.when(to != me_node)
                    def _():
                        start(
                            source, far_ref,
                            pl.ds(pl.multiple_of(peer * ROWS, ROWS) + 2 * rank, 2), rows_at(me_node, 2), far_phase,
                            {"node": to, "period": peer},
                        )

            @pl.when(peer != me_period)
            def _():
                start(
                    source, own_ref, rows_at(peer, rows), rows_at(me_chunk, rows), phase, {"period": peer}
                )

            return 0

        lax.fori_loop(0, chunks, one, 0)
        put(own_ref, me_chunk, tile(source, me_period))

    def spread_nodes(source, target_ref, pitch, rows, phase, same=False):
        def one(k, _):
            peer = across(k)
            start(
                source, target_ref, rows_at(0 if same else peer, rows, pitch), rows_at(me_node, rows, pitch), phase,
                {"node": peer},
            )
            return 0

        lax.fori_loop(0, nodes - 1, one, 0)

    def await_rows(ref, rows, semaphore):
        span = ref.at[pl.ds(0, rows), :]
        pltpu.make_async_copy(span, span, semaphore).wait()

    def put_summary(ref, row, values, pitch=2):
        for rank in range(ranks):
            ref[pl.ds(pitch * rank + row, chunks, stride=ROWS), :] = values[
                rank * chunks : (rank + 1) * chunks
            ]

    def get_summary(ref, row, pitch=2):
        return jnp.concatenate(
            [ref[pl.ds(pitch * rank + row, chunks, stride=ROWS), :] for rank in range(ranks)], axis=0
        )

    def at_period(ref, t):
        return ref[pl.ds(t * tiles, tiles), :]

    def by_node(ref, t, pitch=ROWS):
        return ref[pl.ds(t, tiles, stride=pitch), :]

    def chain_back(values, shares, entering, target_ref):
        for t in reversed(range(ROWS)):
            entering = values(t) + entering
            target_ref[pl.ds(t, tiles, stride=ROWS), :] = entering * (1.0 / horizon)
            entering = entering * at_period(shares, t)

    def passed_back():
        passed = None
        for t in reversed(range(ROWS)):
            value = at_period(duals, t)
            passed = value if passed is None else value + passed
            passed = passed * at_period(kept, t)
        return passed

    def products(share_of, shares, target_ref):
        product = None
        square_sum = None
        for t in range(ROWS):
            share = share_of(t)
            shares[pl.ds(t * tiles, tiles), :] = share
            product = share if product is None else product * share
            target_ref[pl.ds(t * tiles, tiles), :] = product
            square = product * product
            square_sum = square if square_sum is None else square_sum + square
        return product, square_sum

    even = (lax.broadcasted_iota(jnp.int32, (ROWS, LANES), 0) & 1) == 0
    none = jnp.zeros((ROWS, LANES), jnp.float32)

    loads[0].wait()
    loads[1].wait()
    product, square_sum = products(lambda t: by_node(keep, t), kept, grown)
    for t in range(ROWS):
        duals[pl.ds(t * tiles, tiles), :] = by_node(dual, t)
    put_summary(send_a, 0, product)
    put_summary(send_a, 1, passed_back())
    put_summary(send_s, 1, square_sum)

    for k in (2, 3, 4, 5):
        loads[k].wait()

    def pack_one(step, _):
        for k in range(UNROLL):
            d = step * UNROLL + k
            for place, ref in enumerate((cut, cost_cut, keep, dual)):
                pack[rows_at(d * (PACK // ROWS) + place), :] = tile(ref, d)
        return 0

    lax.fori_loop(0, nodes // UNROLL, pack_one, 0)
    cut_tail[...] = cut_tail[...] & (LANES - 1)
    cut_head[...] = cut_head[...] & (LANES - 1)
    pack[pl.ds(4 * ROWS, nodes, stride=PACK), :] = cut_tail[...].astype(jnp.float32)
    pack[pl.ds(4 * ROWS + 1, nodes, stride=PACK), :] = cut_head[...].astype(jnp.float32)

    for k in (8, 9, 10):
        loads[k].wait()

    def square_one(t, sums):
        costs, wanted = sums
        value = tile(target, t)
        wanted = wanted + value * value
        value = tile(cost_prod, t)
        first = value * value
        value = tile(cost_cut, t)
        other = value * value
        for group in range(groups):
            value = tile(cost_inner, group * tiles + t)
            if group % 2:
                first = first + value * value
            else:
                other = other + value * value
        return costs + (first + other), wanted

    costs, wanted = lax.fori_loop(0, tiles, square_one, (none, none))
    first_row = lax.broadcasted_iota(jnp.int32, (ROWS, LANES), 0) < 1
    part[...] = jnp.where(
        first_row, jnp.sum(costs, axis=0, keepdims=True), jnp.sum(wanted, axis=0, keepdims=True)
    )

    pl.semaphore_wait(pltpu.get_barrier_semaphore(), periods + nodes - 2)
    spread_owners(send_a, recv_a, ROWS, 0)
    spread_nodes(part, parts, ROWS, 2, 5, same=True)
    put(parts, me_node, part[...])
    spread_owners(send_s, recv_s, ROWS, 1)
    spread_nodes(pack, packs, PACK, SENT, 2)

    loads[6].wait()
    loads[7].wait()
    tail[...] = tail[...] & (LANES - 1)
    head[...] = head[...] & (LANES - 1)

    def keyed(first, other):
        lane = lax.broadcasted_iota(jnp.int32, first.shape, 1)
        return (first * (LANES * LANES) + other * LANES + lane).astype(jnp.float32)

    keys[pl.ds(0, blocks), :] = keyed(tail[...], head[...])
    keys[pl.ds(blocks, blocks), :] = keyed(head[...], tail[...])
    keys[pl.ds(2 * blocks, nodes), :] = keyed(cut_tail[...], cut_head[...])
    keys[pl.ds(2 * blocks + nodes, nodes), :] = keyed(cut_head[...], cut_tail[...])
    batch = 2 * blocks + 2 * nodes

    def sort_batch(k, _):
        at = pl.ds(pl.multiple_of(k * batch, batch), batch)
        ordered = sort_lanes(keys[at, :]).astype(jnp.int32)
        second[at, :] = lax.shift_right_logical(ordered, 7) & (LANES - 1)
        slot[at, :] = ordered & (LANES - 1)
        return 0

    lax.fori_loop(0, (2 * blocks + 2 * nodes) // batch, sort_batch, 0)

    loads[11].wait()
    loads[12].wait()

    def reorder(step, _):
        moved = []
        for k in range(UNROLL):
            t = step * UNROLL + k
            for group in range(groups):
                j = group * tiles + t
                lanes = lanes_of(slot, j)
                moved.append((flow, j, take(tile(flow, j), lanes)))
                moved.append((cost_inner, j, take(tile(cost_inner, j), lanes)))
            lanes = lanes_of(slot, 2 * blocks + t)
            moved.append((cut, t, take(tile(cut, t), lanes)))
            moved.append((cost_cut, t, take(tile(cost_cut, t), lanes)))
        for ref, number, values in moved:
            put(ref, number, values)
        return 0

    lax.fori_loop(0, tiles // UNROLL, reorder, 0)
    for t in range(ROWS):
        targets[pl.ds(t * tiles, tiles), :] = by_node(target, t)

    await_rows(parts, (nodes - 1) * 2, recv_sem.at[5])
    whole[...] = jnp.where(
        first_row,
        jnp.sum(parts[pl.ds(0, nodes, stride=ROWS), :], axis=0, keepdims=True),
        jnp.sum(parts[pl.ds(1, nodes, stride=ROWS), :], axis=0, keepdims=True),
    )

    def spread_whole(k, _):
        start(whole, wholes, rows_at(0, 2), rows_at(me_period, 2), 12, {"period": around(k)})
        return 0

    lax.fori_loop(0, periods - 1, spread_whole, 0)
    put(wholes, me_period, whole[...])

    await_rows(recv_a, (periods - 1) * ROWS, recv_sem.at[0])
    entering = none
    for j in reversed(range(periods)):
        block = tile(recv_a, j)
        ratio = jnp.where(even, block, pltpu.roll(block, 1, 0))
        put(factor, j, ratio)
        put(give_a, j, entering)
        entering = block + ratio * entering
    give(give_a, ROWS, got_a, 3, far_a, 4)

    await_rows(packs, (nodes - 1) * SENT, recv_sem.at[2])
    packs[rows_at(me_node, PACK, PACK), :] = pack[rows_at(me_node, PACK, PACK), :]
    ends_out[...] = take(
        packs[pl.ds(4 * ROWS + 1, nodes, stride=PACK), :], slot[pl.ds(2 * blocks, nodes), :]
    ).astype(jnp.int32)
    ends_in[...] = take(
        packs[pl.ds(4 * ROWS, nodes, stride=PACK), :], slot[pl.ds(2 * blocks + nodes, nodes), :]
    ).astype(jnp.int32)

    def reorder_back(step, _):
        moved = []
        for k in range(UNROLL):
            d = step * UNROLL + k
            lanes = lanes_of(slot, 2 * blocks + nodes + d)
            for place, ref in enumerate((flow_back, cost_back)):
                moved.append((ref, d, take(tile(packs, d * (PACK // ROWS) + place), lanes)))
        for ref, number, values in moved:
            put(ref, number, values)
        return 0

    lax.fori_loop(0, nodes // UNROLL, reorder_back, 0)
    products(lambda t: packs[pl.ds(2 * ROWS + t, nodes, stride=PACK), :], kept_far, grown_far)

    def update_inner(tau):
        def one(step, _):
            stores = []
            for k in range(UNROLL):
                t = step * UNROLL + k
                here = tile(price, t)
                old = tile(prod, t)
                new = jnp.maximum(old - tau * (tile(cost_prod, t) - here), 0.0)
                stores.append((prod, t, new))
                total = 2.0 * new - old
                for group in range(groups):
                    j = group * tiles + t
                    there = take(tile(price, lax.rem(t + group, tiles)), lanes_of(second, j))
                    old = tile(flow, j)
                    new = jnp.maximum(old - tau * (tile(cost_inner, j) - (there - here)), 0.0)
                    moved = 2.0 * new - old
                    stores.append((flow, j, new))
                    stores.append((change, j, moved))
                    total = total - moved
                stores.append((net, t, total))
            for ref, number, values in stores:
                put(ref, number, values)
            return 0

        lax.fori_loop(0, tiles // UNROLL, one, 0)

    def gather_inner():
        def one(step, _):
            stores = []
            for k in range(UNROLL):
                t = step * UNROLL + k
                total = tile(net, t)
                for group in range(groups):
                    j = group * tiles + lax.rem(t - group + tiles, tiles)
                    total = total + take(tile(change, j), lanes_of(second, blocks + j))
                stores.append((net, t, total))
            for ref, number, values in stores:
                put(ref, number, values)
            return 0

        lax.fori_loop(0, tiles // UNROLL, one, 0)

    def update_cut(tau):
        put(price_far, me_node, tile(price, me_node))

        def one(step, _):
            stores = []
            for k in range(UNROLL):
                t = step * UNROLL + k
                here = tile(price, t)
                other = tile(price_far, t)
                there = take(other, lanes_of(ends_out, t))
                old = tile(cut, t)
                new = jnp.maximum(old - tau * (tile(cost_cut, t) - (there - here)), 0.0)
                stores.append((cut, t, new))
                total = tile(net, t) - (2.0 * new - old)
                there = take(other, lanes_of(ends_in, t))
                old = tile(flow_back, t)
                new = jnp.maximum(old - tau * (tile(cost_back, t) - (here - there)), 0.0)
                stores.append((flow_back, t, new))
                stores.append((net, t, total + (2.0 * new - old)))
            for ref, number, values in stores:
                put(ref, number, values)
            return 0

        lax.fori_loop(0, tiles // UNROLL, one, 0)

    await_rows(got_a, (chunks - 1) * ROWS, recv_sem.at[3])
    chain_back(lambda t: at_period(duals, t), kept, get_summary(got_a, 1), price)
    await_rows(wholes, (periods - 1) * 2, recv_sem.at[12])
    sums = [jnp.sum(wholes[pl.ds(row, periods, stride=ROWS), :], keepdims=True) for row in range(2)]
    omega = jnp.sqrt(sums[0] / sums[1])
    tau = jnp.broadcast_to(ETA / omega, (ROWS, LANES))
    sigma = ETA * omega
    sigma_tile = jnp.broadcast_to(sigma, (ROWS, LANES)) * (1.0 / horizon)
    sigma_wide = jnp.broadcast_to(sigma, (tiles, LANES))
    sigma_stock = sigma_wide * (1.0 / horizon)
    update_inner(tau)
    gather_inner()
    await_rows(far_a, (nodes - 1) * 2, recv_sem.at[4])
    chain_back(
        lambda t: packs[pl.ds(3 * ROWS + t, nodes, stride=PACK), :], kept_far, by_node(far_a, 1), price_far
    )
    update_cut(tau)

    def local_stock(target_ref):
        stock = None
        for t in range(ROWS):
            value = by_node(net, t)
            stock = value if stock is None else at_period(kept, t) * stock + value
            value = at_period(duals, t) + sigma_wide * (at_period(targets, t) - stock * (1.0 / horizon))
            duals[pl.ds(t * tiles, tiles), :] = value
            if target_ref is not None:
                target_ref[pl.ds(t, tiles, stride=ROWS), :] = value
        return stock

    put_summary(send_b, 0, local_stock(late))
    put_summary(send_b, 1, passed_back())
    spread_owners(send_b, recv_b, ROWS, 6)
    spread_nodes(late, lates, ROWS, ROWS, 7)
    await_rows(recv_s, (periods - 1) * ROWS, recv_sem.at[1])
    for j in range(periods):
        factor_c[pl.ds(j * ROWS, ranks), :] = factor[pl.ds(j * ROWS, ranks, stride=2), :]

    await_rows(recv_b, (periods - 1) * ROWS, recv_sem.at[6])
    entering = none
    entered = []
    for j in range(periods):
        entered.append(entering)
        entering = tile(recv_b, j) + tile(factor, j) * entering
    entering = none
    for j in reversed(range(periods)):
        put(give_b, j, jnp.where(even, entered[j], entering))
        answer = tile(recv_b, j) - sigma_tile * tile(recv_s, j) * pltpu.roll(entered[j], 1, 0)
        entering = answer + tile(factor, j) * entering
    give(give_b, ROWS, got_b, 8, far_b, 9)

    await_rows(got_b, (chunks - 1) * ROWS, recv_sem.at[8])
    stock = get_summary(got_b, 0) * sigma_stock
    for t in range(ROWS):
        duals[pl.ds(t * tiles, tiles), :] = at_period(duals, t) - at_period(grown, t) * stock
    chain_back(lambda t: at_period(duals, t), kept, get_summary(got_b, 1), price)
    update_inner(tau)
    gather_inner()
    await_rows(lates, (nodes - 1) * ROWS, recv_sem.at[7])
    await_rows(far_b, (nodes - 1) * 2, recv_sem.at[9])
    stock_far = by_node(far_b, 0) * sigma_stock
    chain_back(
        lambda t: by_node(lates, t) - at_period(grown_far, t) * stock_far, kept_far, by_node(far_b, 1), price_far
    )
    update_cut(tau)
    put_summary(send_c, 0, local_stock(None), 1)
    spread_owners(send_c, recv_c, ranks, 10)

    def restore(step, _):
        moved = []
        for k in range(UNROLL):
            t = step * UNROLL + k
            for group in range(groups):
                j = group * tiles + t
                moved.append((flow, j, take(tile(flow, j), lanes_of(tail, j))))
            moved.append((cut, t, take(tile(cut, t), lanes_of(cut_tail, t))))
        for ref, number, values in moved:
            put(ref, number, values)
        return 0

    lax.fori_loop(0, tiles // UNROLL, restore, 0)

    await_rows(recv_c, (periods - 1) * ranks, recv_sem.at[10])
    entering = jnp.zeros((ranks, LANES), jnp.float32)
    for j in range(periods):
        give_c[pl.ds(j * ROWS, ranks), :] = entering
        entering = recv_c[pl.ds(j * ROWS, ranks), :] + factor_c[pl.ds(j * ROWS, ranks), :] * entering
    give(give_c, ranks, got_c, 11)
    await_rows(got_c, (chunks - 1) * ranks, recv_sem.at[11])
    stock = get_summary(got_c, 0, 1) * sigma_stock
    for t in range(ROWS):
        dual[pl.ds(t, tiles, stride=ROWS), :] = at_period(duals, t) - at_period(grown, t) * stock

    for phase, rows in (
        (0, (periods - 1) * ROWS),
        (1, (periods - 1) * ROWS),
        (2, (nodes - 1) * SENT),
        (3, (chunks - 1) * ROWS),
        (5, (nodes - 1) * 2),
        (12, (periods - 1) * 2),
        (6, (periods - 1) * ROWS),
        (7, (nodes - 1) * ROWS),
        (8, (chunks - 1) * ROWS),
        (10, (periods - 1) * ranks),
        (11, (chunks - 1) * ranks),
    ):
        await_rows(packs, rows, send_sem.at[phase])
    for phase in (4, 9):
        await_rows(packs, chunks * (ranks - 1) * 2, send_sem.at[phase])

        @pl.when(me_chunk != node_chunk)
        def _():
            await_rows(packs, chunks * 2, send_sem.at[phase])


def hand_over(count, *refs):
    semaphores = refs[-1]
    copies = [
        pltpu.make_async_copy(refs[k], refs[count + k], semaphores.at[k]) for k in range(count)
    ]
    for copy in copies:
        copy.start()
    for copy in copies:
        copy.wait()


def solution(mesh):
    nodes, periods = mesh.shape["node"], mesh.shape["period"]

    def to_tiles(values):
        rows, columns = values.shape
        return values.reshape(rows, columns // LANES, LANES).transpose(1, 0, 2).reshape(-1, LANES)

    def from_tiles(values):
        count = values.shape[0] // ROWS
        return values.reshape(count, ROWS, LANES).transpose(1, 0, 2).reshape(ROWS, count * LANES)

    def body(*operands):
        floats = [to_tiles(values) for values in operands[:9]]
        indices = [values.reshape(-1, LANES) for values in operands[9:]]
        tiles = floats[0].shape[0] // ROWS
        groups = floats[1].shape[0] // floats[0].shape[0]
        blocks = tiles * groups
        slab = (tiles * ROWS, LANES)
        arcs = (blocks * ROWS, LANES)
        ring = (periods * ROWS, LANES)
        sorts = (2 * blocks + 2 * nodes, LANES)

        def room(shape, kind=jnp.float32):
            return pltpu.VMEM(shape, kind)

        scratch = [
            room(slab), room(arcs), room(slab), room(slab), room(slab),
            room((blocks, LANES), jnp.int32), room((blocks, LANES), jnp.int32),
            room((tiles, LANES), jnp.int32), room((tiles, LANES), jnp.int32),
            room(slab), room(slab), room(slab), room(slab), room(slab), room(slab),
            room(slab), room(slab), room(slab), room(arcs),
            room(sorts), room(sorts, jnp.int32), room(sorts, jnp.int32),
            room((nodes, LANES), jnp.int32), room((nodes, LANES), jnp.int32),
            room((nodes * PACK, LANES)), room((nodes * PACK, LANES)), room(slab), room(slab),
            room(slab), room(slab), room((ROWS, LANES)), room(slab), room((ROWS, LANES)), room(ring),
            room(ring), room(ring), room(ring), room(ring), room(slab), room(ring), room(ring),
            room(ring), room(ring), room(ring), room(ring), room(slab),
            room(ring), room(ring), room(ring), room(ring),
            room(ring), room(ring),
            pltpu.SemaphoreType.DMA((13,)),
            pltpu.SemaphoreType.DMA((13,)),
            pltpu.SemaphoreType.DMA((13,)),
        ]
        anywhere = pl.BlockSpec(memory_space=pl.ANY)
        inside = pl.BlockSpec(memory_space=pltpu.VMEM)
        shapes = (slab, arcs, slab, slab)
        results = pl.pallas_call(
            functools.partial(kernel, (nodes, periods, tiles, groups)),
            out_shape=[pltpu.VMEM(shape, jnp.float32) for shape in shapes],
            in_specs=[anywhere] * 13,
            out_specs=[inside] * 4,
            scratch_shapes=scratch,
            compiler_params=pltpu.CompilerParams(
                collective_id=0, has_side_effects=True, vmem_limit_bytes=LIMIT
            ),
        )(*floats, *indices)
        outputs = pl.pallas_call(
            functools.partial(hand_over, 4),
            out_shape=[jax.ShapeDtypeStruct(shape, jnp.float32) for shape in shapes],
            in_specs=[anywhere] * 4,
            out_specs=[anywhere] * 4,
            scratch_shapes=[pltpu.SemaphoreType.DMA((4,))],
            compiler_params=pltpu.CompilerParams(vmem_limit_bytes=LIMIT // 8),
        )(*results)
        return tuple(from_tiles(values) for values in outputs)

    both, node = P("period", "node"), P("node")
    return jax.shard_map(
        body,
        mesh=mesh,
        in_specs=(both,) * 9 + (node,) * 4,
        out_specs=(both,) * 4,
        check_vma=False,
    )
```

```python
import functools

import jax
import jax.numpy as jnp
from jax import lax
from jax.experimental import pallas as pl
from jax.experimental.pallas import tpu as pltpu
from jax.sharding import PartitionSpec as P

MESH = pl.DeviceIdType.MESH
ETA = 0.25
LANES = 128
ROWS = 8
PACK = 40
SENT = 34
UNROLL = 16
LIMIT = 56 * 1024 * 1024


def take(values, lanes):
    return jnp.take_along_axis(values, lanes, axis=1, mode="promise_in_bounds")


def sort_lanes(values):
    lane = lax.broadcasted_iota(jnp.int32, values.shape, 1)
    size = 2
    while size <= LANES:
        step = size // 2
        while step:
            other = take(values, lane ^ step)
            low = ((lane & size) == 0) == ((lane & step) == 0)
            values = jnp.where(low, jnp.minimum(values, other), jnp.maximum(values, other))
            step //= 2
        size *= 2
    return values


def kernel(sizes, *refs):
    nodes, periods, tiles, groups = sizes
    (
        prod_in, flow_in, cut_in, dual_in, cost_prod_in, cost_inner_in, cost_cut_in, target_in, keep_in,
        tail_in, head_in, cut_tail_in, cut_head_in,
        prod, flow, cut, dual,
        cost_prod, cost_inner, cost_cut, target, keep,
        tail, head, cut_tail, cut_head,
        kept, duals, targets, grown, kept_far, grown_far,
        price, price_far, net, change,
        keys, second, slot, ends_out, ends_in,
        pack, packs, flow_back, cost_back,
        late, lates, part, parts, whole, wholes,
        send_a, recv_a, give_a, got_a, far_a, send_s, recv_s,
        send_b, recv_b, give_b, got_b, far_b,
        send_c, recv_c, give_c, got_c,
        factor, factor_c,
        in_sem, send_sem, recv_sem, send_sem_c, recv_sem_c,
    ) = refs
    me_node = lax.axis_index("node")
    me_period = lax.axis_index("period")
    horizon = periods * ROWS
    blocks = groups * tiles
    chunks = periods // 2
    quarters = chunks // 2
    ranks = tiles // chunks
    me_chunk = lax.rem(me_period, chunks)

    def rows_at(number, rows=ROWS, pitch=ROWS):
        return pl.ds(pl.multiple_of(number * pitch, ROWS), rows)

    def tile(ref, number):
        return ref[rows_at(number), :]

    def put(ref, number, values):
        ref[rows_at(number), :] = values

    def lanes_of(ref, number):
        return jnp.broadcast_to(ref[pl.ds(number, 1), :], (ROWS, LANES))

    loads = [
        pltpu.make_async_copy(source, target_ref, in_sem.at[k])
        for k, (source, target_ref) in enumerate(
            (
                (keep_in, keep),
                (dual_in, dual),
                (cut_tail_in, cut_tail),
                (cut_head_in, cut_head),
                (cut_in, cut),
                (cost_cut_in, cost_cut),
                (tail_in, tail),
                (head_in, head),
                (target_in, target),
                (cost_prod_in, cost_prod),
                (cost_inner_in, cost_inner),
                (flow_in, flow),
                (prod_in, prod),
            )
        )
    ]
    def greet(device):
        pl.semaphore_signal(
            pltpu.get_barrier_semaphore(), inc=1, device_id=device, device_id_type=MESH
        )

    def around(i):
        return lax.rem(
            me_period + periods // 2 + (1 - 2 * lax.rem(i, 2)) * lax.div(i + 1, 2), periods
        )

    def away(i):
        return lax.rem(2 + i + lax.div(i, 2) + 2 * lax.div(i, 3), 4)

    def across(k):
        y = lax.rem(lax.div(me_node, 8) + away(lax.div(k, 8)), 4)
        x = lax.rem(lax.div(me_node, 2) + away(lax.rem(lax.div(k, 2), 4)), 4)
        return y * 8 + x * 2 + lax.rem(me_node + 1 + k, 2)

    def greet_period(k, _):
        greet({"period": around(k)})
        return 0

    def greet_node(k, _):
        greet({"node": across(k)})
        return 0

    node_chunk = lax.rem(me_node, chunks)

    for load in loads[:2]:
        load.start()
    lax.fori_loop(0, periods - 1, greet_period, 0)
    for load in loads[2:]:
        load.start()
    lax.fori_loop(0, nodes - 1, greet_node, 0)

    def start(source, target_ref, source_rows, target_rows, phase, device):
        pltpu.make_async_remote_copy(
            src_ref=source.at[source_rows, :],
            dst_ref=target_ref.at[target_rows, :],
            send_sem=send_sem.at[phase],
            recv_sem=recv_sem.at[phase],
            device_id=device,
            device_id_type=MESH,
        ).start()

    def spread_owners(source, target_ref, phase):
        def one(k, _):
            peer = around(k)
            start(
                source, target_ref, rows_at(lax.rem(peer, chunks)), rows_at(me_period), phase, {"period": peer}
            )
            return 0

        lax.fori_loop(0, periods - 1, one, 0)
        put(target_ref, me_period, tile(source, me_chunk))

    def give(source, count, own_ref, phase, far_ref=None, far_phase=None):
        place = lax.rem(me_period, count)

        def one(i, _):
            pair = lax.div(i, 2)
            peer = lax.rem(
                me_period + periods - count // 2 + pair + lax.rem(i, 2) * (count - 1 - 2 * pair), periods
            )
            if far_ref is not None:
                for rank in range(ranks):
                    to = me_chunk + rank * chunks

                    @pl.when(to != me_node)
                    def _():
                        start(
                            source, far_ref,
                            pl.ds(pl.multiple_of(peer * ROWS, ROWS) + 2 * rank, 2), rows_at(me_node, 2), far_phase,
                            {"node": to, "period": peer},
                        )

            @pl.when(peer != me_period)
            def _():
                start(source, own_ref, rows_at(peer), rows_at(place), phase, {"period": peer})

            return 0

        lax.fori_loop(0, count, one, 0)
        put(own_ref, place, tile(source, me_period))

    def spread_nodes(source, target_ref, pitch, rows, phase, same=False):
        def one(k, _):
            peer = across(k)
            start(
                source, target_ref, rows_at(0 if same else peer, rows, pitch), rows_at(me_node, rows, pitch), phase,
                {"node": peer},
            )
            return 0

        lax.fori_loop(0, nodes - 1, one, 0)

    def await_rows(ref, rows, semaphore):
        span = ref.at[pl.ds(0, rows), :]
        pltpu.make_async_copy(span, span, semaphore).wait()

    def put_summary(ref, row, values):
        for rank in range(ranks):
            ref[pl.ds(2 * rank + row, chunks, stride=ROWS), :] = values[rank * chunks : (rank + 1) * chunks]

    def get_summary(ref, row):
        return jnp.concatenate(
            [ref[pl.ds(2 * rank + row, chunks, stride=ROWS), :] for rank in range(ranks)], axis=0
        )

    def put_quarters(ref, values):
        for row in range(2 * ranks):
            ref[pl.ds(row, quarters, stride=ROWS), :] = values[row * quarters : (row + 1) * quarters]

    def get_quarters(ref):
        return jnp.concatenate(
            [ref[pl.ds(row, quarters, stride=ROWS), :] for row in range(2 * ranks)], axis=0
        )

    def at_period(ref, t):
        return ref[pl.ds(t * tiles, tiles), :]

    def by_node(ref, t, pitch=ROWS):
        return ref[pl.ds(t, tiles, stride=pitch), :]

    def chain_back(values, shares, entering, target_ref):
        for t in reversed(range(ROWS)):
            entering = values(t) + entering
            target_ref[pl.ds(t, tiles, stride=ROWS), :] = entering * (1.0 / horizon)
            entering = entering * at_period(shares, t)

    def passed_back():
        passed = None
        for t in reversed(range(ROWS)):
            value = at_period(duals, t)
            passed = value if passed is None else value + passed
            passed = passed * at_period(kept, t)
        return passed

    def products(share_of, shares, target_ref):
        product = None
        square_sum = None
        for t in range(ROWS):
            share = share_of(t)
            shares[pl.ds(t * tiles, tiles), :] = share
            product = share if product is None else product * share
            target_ref[pl.ds(t * tiles, tiles), :] = product
            square = product * product
            square_sum = square if square_sum is None else square_sum + square
        return product, square_sum

    even = (lax.broadcasted_iota(jnp.int32, (ROWS, LANES), 0) & 1) == 0
    none = jnp.zeros((ROWS, LANES), jnp.float32)

    loads[0].wait()
    loads[1].wait()
    product, square_sum = products(lambda t: by_node(keep, t), kept, grown)
    for t in range(ROWS):
        duals[pl.ds(t * tiles, tiles), :] = by_node(dual, t)
    put_summary(send_a, 0, product)
    put_summary(send_a, 1, passed_back())
    put_summary(send_s, 1, square_sum)
    put_summary(
        send_s,
        0,
        jnp.concatenate(
            [
                pltpu.roll(product[rank * chunks : (rank + 1) * chunks], quarters, 0)
                for rank in range(ranks)
            ],
            axis=0,
        ),
    )

    for k in (2, 3, 4, 5):
        loads[k].wait()

    def pack_one(step, _):
        for k in range(UNROLL):
            d = step * UNROLL + k
            for place, ref in enumerate((cut, cost_cut, keep, dual)):
                pack[rows_at(d * (PACK // ROWS) + place), :] = tile(ref, d)
        return 0

    lax.fori_loop(0, nodes // UNROLL, pack_one, 0)
    cut_tail[...] = cut_tail[...] & (LANES - 1)
    cut_head[...] = cut_head[...] & (LANES - 1)
    pack[pl.ds(4 * ROWS, nodes, stride=PACK), :] = cut_tail[...].astype(jnp.float32)
    pack[pl.ds(4 * ROWS + 1, nodes, stride=PACK), :] = cut_head[...].astype(jnp.float32)

    for k in (8, 9, 10):
        loads[k].wait()

    def square_one(t, sums):
        costs, wanted = sums
        value = tile(target, t)
        wanted = wanted + value * value
        value = tile(cost_prod, t)
        first = value * value
        value = tile(cost_cut, t)
        other = value * value
        for group in range(groups):
            value = tile(cost_inner, group * tiles + t)
            if group % 2:
                first = first + value * value
            else:
                other = other + value * value
        return costs + (first + other), wanted

    costs, wanted = lax.fori_loop(0, tiles, square_one, (none, none))
    first_row = lax.broadcasted_iota(jnp.int32, (ROWS, LANES), 0) < 1
    part[...] = jnp.where(
        first_row, jnp.sum(costs, axis=0, keepdims=True), jnp.sum(wanted, axis=0, keepdims=True)
    )

    pl.semaphore_wait(pltpu.get_barrier_semaphore(), periods + nodes - 2)
    spread_owners(send_a, recv_a, 0)
    spread_nodes(part, parts, ROWS, 2, 5, same=True)
    put(parts, me_node, part[...])
    spread_owners(send_s, recv_s, 1)
    spread_nodes(pack, packs, PACK, SENT, 2)

    loads[6].wait()
    loads[7].wait()
    tail[...] = tail[...] & (LANES - 1)
    head[...] = head[...] & (LANES - 1)

    def keyed(first, other):
        lane = lax.broadcasted_iota(jnp.int32, first.shape, 1)
        return (first * (LANES * LANES) + other * LANES + lane).astype(jnp.float32)

    keys[pl.ds(0, blocks), :] = keyed(tail[...], head[...])
    keys[pl.ds(blocks, blocks), :] = keyed(head[...], tail[...])
    keys[pl.ds(2 * blocks, nodes), :] = keyed(cut_tail[...], cut_head[...])
    keys[pl.ds(2 * blocks + nodes, nodes), :] = keyed(cut_head[...], cut_tail[...])
    batch = 2 * blocks + 2 * nodes

    def sort_batch(k, _):
        at = pl.ds(pl.multiple_of(k * batch, batch), batch)
        ordered = sort_lanes(keys[at, :]).astype(jnp.int32)
        second[at, :] = lax.shift_right_logical(ordered, 7) & (LANES - 1)
        slot[at, :] = ordered & (LANES - 1)
        return 0

    lax.fori_loop(0, (2 * blocks + 2 * nodes) // batch, sort_batch, 0)

    loads[11].wait()
    loads[12].wait()

    def reorder(step, _):
        moved = []
        for k in range(UNROLL):
            t = step * UNROLL + k
            for group in range(groups):
                j = group * tiles + t
                lanes = lanes_of(slot, j)
                moved.append((flow, j, take(tile(flow, j), lanes)))
                moved.append((cost_inner, j, take(tile(cost_inner, j), lanes)))
            lanes = lanes_of(slot, 2 * blocks + t)
            moved.append((cut, t, take(tile(cut, t), lanes)))
            moved.append((cost_cut, t, take(tile(cost_cut, t), lanes)))
        for ref, number, values in moved:
            put(ref, number, values)
        return 0

    lax.fori_loop(0, tiles // UNROLL, reorder, 0)
    for t in range(ROWS):
        targets[pl.ds(t * tiles, tiles), :] = by_node(target, t)

    await_rows(parts, (nodes - 1) * 2, recv_sem.at[5])
    whole[...] = jnp.where(
        first_row,
        jnp.sum(parts[pl.ds(0, nodes, stride=ROWS), :], axis=0, keepdims=True),
        jnp.sum(parts[pl.ds(1, nodes, stride=ROWS), :], axis=0, keepdims=True),
    )

    def spread_whole(k, _):
        start(whole, wholes, rows_at(0, 2), rows_at(me_period, 2), 12, {"period": around(k)})
        return 0

    lax.fori_loop(0, periods - 1, spread_whole, 0)
    put(wholes, me_period, whole[...])

    await_rows(recv_a, (periods - 1) * ROWS, recv_sem.at[0])
    entering = none
    for j in reversed(range(periods)):
        block = tile(recv_a, j)
        ratio = jnp.where(even, block, pltpu.roll(block, 1, 0))
        put(factor, j, ratio)
        put(give_a, j, entering)
        entering = block + ratio * entering
    give(give_a, chunks, got_a, 3, far_a, 4)

    await_rows(packs, (nodes - 1) * SENT, recv_sem.at[2])
    packs[rows_at(me_node, PACK, PACK), :] = pack[rows_at(me_node, PACK, PACK), :]
    ends_out[...] = take(
        packs[pl.ds(4 * ROWS + 1, nodes, stride=PACK), :], slot[pl.ds(2 * blocks, nodes), :]
    ).astype(jnp.int32)
    ends_in[...] = take(
        packs[pl.ds(4 * ROWS, nodes, stride=PACK), :], slot[pl.ds(2 * blocks + nodes, nodes), :]
    ).astype(jnp.int32)

    def reorder_back(step, _):
        moved = []
        for k in range(UNROLL):
            d = step * UNROLL + k
            lanes = lanes_of(slot, 2 * blocks + nodes + d)
            for place, ref in enumerate((flow_back, cost_back)):
                moved.append((ref, d, take(tile(packs, d * (PACK // ROWS) + place), lanes)))
        for ref, number, values in moved:
            put(ref, number, values)
        return 0

    lax.fori_loop(0, nodes // UNROLL, reorder_back, 0)
    products(lambda t: packs[pl.ds(2 * ROWS + t, nodes, stride=PACK), :], kept_far, grown_far)

    def update_inner(tau):
        def one(step, _):
            stores = []
            for k in range(UNROLL):
                t = step * UNROLL + k
                here = tile(price, t)
                old = tile(prod, t)
                new = jnp.maximum(old - tau * (tile(cost_prod, t) - here), 0.0)
                stores.append((prod, t, new))
                total = 2.0 * new - old
                for group in range(groups):
                    j = group * tiles + t
                    there = take(tile(price, lax.rem(t + group, tiles)), lanes_of(second, j))
                    old = tile(flow, j)
                    new = jnp.maximum(old - tau * (tile(cost_inner, j) - (there - here)), 0.0)
                    moved = 2.0 * new - old
                    stores.append((flow, j, new))
                    stores.append((change, j, moved))
                    total = total - moved
                stores.append((net, t, total))
            for ref, number, values in stores:
                put(ref, number, values)
            return 0

        lax.fori_loop(0, tiles // UNROLL, one, 0)

    def gather_inner():
        def one(step, _):
            stores = []
            for k in range(UNROLL):
                t = step * UNROLL + k
                total = tile(net, t)
                for group in range(groups):
                    j = group * tiles + lax.rem(t - group + tiles, tiles)
                    total = total + take(tile(change, j), lanes_of(second, blocks + j))
                stores.append((net, t, total))
            for ref, number, values in stores:
                put(ref, number, values)
            return 0

        lax.fori_loop(0, tiles // UNROLL, one, 0)

    def update_cut(tau):
        put(price_far, me_node, tile(price, me_node))

        def one(step, _):
            stores = []
            for k in range(UNROLL):
                t = step * UNROLL + k
                here = tile(price, t)
                other = tile(price_far, t)
                there = take(other, lanes_of(ends_out, t))
                old = tile(cut, t)
                new = jnp.maximum(old - tau * (tile(cost_cut, t) - (there - here)), 0.0)
                stores.append((cut, t, new))
                total = tile(net, t) - (2.0 * new - old)
                there = take(other, lanes_of(ends_in, t))
                old = tile(flow_back, t)
                new = jnp.maximum(old - tau * (tile(cost_back, t) - (here - there)), 0.0)
                stores.append((flow_back, t, new))
                stores.append((net, t, total + (2.0 * new - old)))
            for ref, number, values in stores:
                put(ref, number, values)
            return 0

        lax.fori_loop(0, tiles // UNROLL, one, 0)

    await_rows(got_a, (chunks - 1) * ROWS, recv_sem.at[3])
    chain_back(lambda t: at_period(duals, t), kept, get_summary(got_a, 1), price)
    await_rows(wholes, (periods - 1) * 2, recv_sem.at[12])
    sums = [jnp.sum(wholes[pl.ds(row, periods, stride=ROWS), :], keepdims=True) for row in range(2)]
    omega = jnp.sqrt(sums[0] / sums[1])
    tau = jnp.broadcast_to(ETA / omega, (ROWS, LANES))
    sigma = ETA * omega
    sigma_tile = jnp.broadcast_to(sigma, (ROWS, LANES)) * (1.0 / horizon)
    sigma_wide = jnp.broadcast_to(sigma, (tiles, LANES))
    sigma_stock = sigma_wide * (1.0 / horizon)
    update_inner(tau)
    gather_inner()
    await_rows(far_a, (nodes - 1) * 2, recv_sem.at[4])
    chain_back(
        lambda t: packs[pl.ds(3 * ROWS + t, nodes, stride=PACK), :], kept_far, by_node(far_a, 1), price_far
    )
    update_cut(tau)

    def local_stock(target_ref):
        stock = None
        for t in range(ROWS):
            value = by_node(net, t)
            stock = value if stock is None else at_period(kept, t) * stock + value
            value = at_period(duals, t) + sigma_wide * (at_period(targets, t) - stock * (1.0 / horizon))
            duals[pl.ds(t * tiles, tiles), :] = value
            if target_ref is not None:
                target_ref[pl.ds(t, tiles, stride=ROWS), :] = value
        return stock

    put_summary(send_b, 0, local_stock(late))
    put_summary(send_b, 1, passed_back())
    spread_owners(send_b, recv_b, 6)
    spread_nodes(late, lates, ROWS, ROWS, 7)
    await_rows(recv_s, (periods - 1) * ROWS, recv_sem.at[1])
    for j in range(periods):
        other = tile(recv_s, j)
        ratio = tile(factor, j)
        low = jnp.where(even, ratio, pltpu.roll(other, 1, 0))
        put(factor_c, j, jnp.where(me_chunk < quarters, low, jnp.where(even, other, ratio)))

    await_rows(recv_b, (periods - 1) * ROWS, recv_sem.at[6])
    entering = none
    entered = []
    for j in range(periods):
        entered.append(entering)
        entering = tile(recv_b, j) + tile(factor, j) * entering
    entering = none
    for j in reversed(range(periods)):
        put(give_b, j, jnp.where(even, entered[j], entering))
        answer = tile(recv_b, j) - sigma_tile * tile(recv_s, j) * pltpu.roll(entered[j], 1, 0)
        entering = answer + tile(factor, j) * entering
    give(give_b, chunks, got_b, 8, far_b, 9)

    await_rows(got_b, (chunks - 1) * ROWS, recv_sem.at[8])
    stock = get_summary(got_b, 0) * sigma_stock
    for t in range(ROWS):
        duals[pl.ds(t * tiles, tiles), :] = at_period(duals, t) - at_period(grown, t) * stock
    chain_back(lambda t: at_period(duals, t), kept, get_summary(got_b, 1), price)
    update_inner(tau)
    gather_inner()
    await_rows(lates, (nodes - 1) * ROWS, recv_sem.at[7])
    await_rows(far_b, (nodes - 1) * 2, recv_sem.at[9])
    stock_far = by_node(far_b, 0) * sigma_stock
    chain_back(
        lambda t: by_node(lates, t) - at_period(grown_far, t) * stock_far, kept_far, by_node(far_b, 1), price_far
    )
    update_cut(tau)
    put_quarters(send_c, local_stock(None))

    def spread_later(k, _):
        peer = around(k)

        @pl.when(jnp.logical_and(me_period < periods - 1, jnp.logical_or(me_period < peer, peer < 2)))
        def _():
            pltpu.make_async_remote_copy(
                src_ref=send_c.at[rows_at(lax.rem(peer, quarters)), :],
                dst_ref=recv_c.at[rows_at(me_period), :],
                send_sem=send_sem_c.at[peer],
                recv_sem=recv_sem_c.at[me_period],
                device_id={"period": peer},
                device_id_type=MESH,
            ).start()

        return 0

    lax.fori_loop(0, periods - 1, spread_later, 0)
    put(recv_c, me_period, tile(send_c, lax.rem(me_period, quarters)))

    def restore(step, _):
        moved = []
        for k in range(UNROLL):
            t = step * UNROLL + k
            for group in range(groups):
                j = group * tiles + t
                moved.append((flow, j, take(tile(flow, j), lanes_of(tail, j))))
            moved.append((cut, t, take(tile(cut, t), lanes_of(cut_tail, t))))
        for ref, number, values in moved:
            put(ref, number, values)
        return 0

    lax.fori_loop(0, tiles // UNROLL, restore, 0)

    def await_earlier(j, _):
        @pl.when(
            jnp.logical_and(
                jnp.logical_and(j < periods - 1, j != me_period),
                jnp.logical_or(j < me_period, me_period < 2),
            )
        )
        def _():
            await_rows(packs, ROWS, recv_sem_c.at[j])

        return 0

    lax.fori_loop(0, periods, await_earlier, 0)
    entering = none
    for j in range(periods):
        put(give_c, j, entering)
        entering = tile(recv_c, j) + tile(factor_c, j) * entering
    give(give_c, quarters, got_c, 11)
    await_rows(got_c, (quarters - 1) * ROWS, recv_sem.at[11])
    stock = get_quarters(got_c) * sigma_stock
    for t in range(ROWS):
        dual[pl.ds(t, tiles, stride=ROWS), :] = at_period(duals, t) - at_period(grown, t) * stock

    for phase, rows in (
        (0, (periods - 1) * ROWS),
        (1, (periods - 1) * ROWS),
        (2, (nodes - 1) * SENT),
        (3, (chunks - 1) * ROWS),
        (5, (nodes - 1) * 2),
        (12, (periods - 1) * 2),
        (6, (periods - 1) * ROWS),
        (7, (nodes - 1) * ROWS),
        (8, (chunks - 1) * ROWS),
        (11, (quarters - 1) * ROWS),
    ):
        await_rows(packs, rows, send_sem.at[phase])

    def await_sent(k, _):
        peer = around(k)

        @pl.when(jnp.logical_and(me_period < periods - 1, jnp.logical_or(me_period < peer, peer < 2)))
        def _():
            await_rows(packs, ROWS, send_sem_c.at[peer])

        return 0

    lax.fori_loop(0, periods - 1, await_sent, 0)
    for phase in (4, 9):
        await_rows(packs, chunks * (ranks - 1) * 2, send_sem.at[phase])

        @pl.when(me_chunk != node_chunk)
        def _():
            await_rows(packs, chunks * 2, send_sem.at[phase])


def hand_over(count, *refs):
    semaphores = refs[-1]
    copies = [
        pltpu.make_async_copy(refs[k], refs[count + k], semaphores.at[k]) for k in range(count)
    ]
    for copy in copies:
        copy.start()
    for copy in copies:
        copy.wait()


def solution(mesh):
    nodes, periods = mesh.shape["node"], mesh.shape["period"]

    def to_tiles(values):
        rows, columns = values.shape
        return values.reshape(rows, columns // LANES, LANES).transpose(1, 0, 2).reshape(-1, LANES)

    def from_tiles(values):
        count = values.shape[0] // ROWS
        return values.reshape(count, ROWS, LANES).transpose(1, 0, 2).reshape(ROWS, count * LANES)

    def body(*operands):
        floats = [to_tiles(values) for values in operands[:9]]
        indices = [values.reshape(-1, LANES) for values in operands[9:]]
        tiles = floats[0].shape[0] // ROWS
        groups = floats[1].shape[0] // floats[0].shape[0]
        blocks = tiles * groups
        slab = (tiles * ROWS, LANES)
        arcs = (blocks * ROWS, LANES)
        ring = (periods * ROWS, LANES)
        sorts = (2 * blocks + 2 * nodes, LANES)

        def room(shape, kind=jnp.float32):
            return pltpu.VMEM(shape, kind)

        scratch = [
            room(slab), room(arcs), room(slab), room(slab), room(slab),
            room((blocks, LANES), jnp.int32), room((blocks, LANES), jnp.int32),
            room((tiles, LANES), jnp.int32), room((tiles, LANES), jnp.int32),
            room(slab), room(slab), room(slab), room(slab), room(slab), room(slab),
            room(slab), room(slab), room(slab), room(arcs),
            room(sorts), room(sorts, jnp.int32), room(sorts, jnp.int32),
            room((nodes, LANES), jnp.int32), room((nodes, LANES), jnp.int32),
            room((nodes * PACK, LANES)), room((nodes * PACK, LANES)), room(slab), room(slab),
            room(slab), room(slab), room((ROWS, LANES)), room(slab), room((ROWS, LANES)), room(ring),
            room(ring), room(ring), room(ring), room(ring), room(slab), room(ring), room(ring),
            room(ring), room(ring), room(ring), room(ring), room(slab),
            room(ring), room(ring), room(ring), room(ring),
            room(ring), room(ring),
            pltpu.SemaphoreType.DMA((13,)),
            pltpu.SemaphoreType.DMA((13,)),
            pltpu.SemaphoreType.DMA((13,)),
            pltpu.SemaphoreType.DMA((periods,)),
            pltpu.SemaphoreType.DMA((periods,)),
        ]
        anywhere = pl.BlockSpec(memory_space=pl.ANY)
        inside = pl.BlockSpec(memory_space=pltpu.VMEM)
        shapes = (slab, arcs, slab, slab)
        results = pl.pallas_call(
            functools.partial(kernel, (nodes, periods, tiles, groups)),
            out_shape=[pltpu.VMEM(shape, jnp.float32) for shape in shapes],
            in_specs=[anywhere] * 13,
            out_specs=[inside] * 4,
            scratch_shapes=scratch,
            compiler_params=pltpu.CompilerParams(
                collective_id=0, has_side_effects=True, vmem_limit_bytes=LIMIT
            ),
        )(*floats, *indices)
        outputs = pl.pallas_call(
            functools.partial(hand_over, 4),
            out_shape=[jax.ShapeDtypeStruct(shape, jnp.float32) for shape in shapes],
            in_specs=[anywhere] * 4,
            out_specs=[anywhere] * 4,
            scratch_shapes=[pltpu.SemaphoreType.DMA((4,))],
            compiler_params=pltpu.CompilerParams(vmem_limit_bytes=LIMIT // 8),
        )(*results)
        return tuple(from_tiles(values) for values in outputs)

    both, node = P("period", "node"), P("node")
    return jax.shard_map(
        body,
        mesh=mesh,
        in_specs=(both,) * 9 + (node,) * 4,
        out_specs=(both,) * 4,
        check_vma=False,
    )
```

```python
import functools

import jax
import jax.numpy as jnp
from jax import lax
from jax.experimental import pallas as pl
from jax.experimental.pallas import tpu as pltpu
from jax.sharding import PartitionSpec as P

MESH = pl.DeviceIdType.MESH
ETA = 0.25
LANES = 128
ROWS = 8
PACK = 40
SENT = 34
UNROLL = 16
LIMIT = 56 * 1024 * 1024


def take(values, lanes):
    return jnp.take_along_axis(values, lanes, axis=1, mode="promise_in_bounds")


def sort_lanes(values):
    lane = lax.broadcasted_iota(jnp.int32, values.shape, 1)
    size = 2
    while size <= LANES:
        step = size // 2
        while step:
            other = take(values, lane ^ step)
            low = ((lane & size) == 0) == ((lane & step) == 0)
            values = jnp.where(low, jnp.minimum(values, other), jnp.maximum(values, other))
            step //= 2
        size *= 2
    return values


def kernel(sizes, *refs):
    nodes, periods, tiles, groups = sizes
    (
        prod_in, flow_in, cut_in, dual_in, cost_prod_in, cost_inner_in, cost_cut_in, target_in, keep_in,
        tail_in, head_in, cut_tail_in, cut_head_in,
        prod, flow, cut, dual,
        cost_prod, cost_inner, cost_cut, target, keep,
        tail, head, cut_tail, cut_head,
        kept, duals, targets, grown, kept_far, grown_far,
        price, price_far, net, change,
        keys, second, slot, ends_out, ends_in,
        pack, packs, flow_back, cost_back,
        late, lates, part, parts, whole, wholes,
        send_a, recv_a, give_a, got_a, far_a, send_s, recv_s,
        send_b, recv_b, give_b, got_b, far_b,
        send_c, recv_c, give_c, got_c,
        factor, factor_c,
        in_sem, send_sem, recv_sem, send_sem_c, recv_sem_c,
    ) = refs
    me_node = lax.axis_index("node")
    me_period = lax.axis_index("period")
    horizon = periods * ROWS
    blocks = groups * tiles
    chunks = periods // 2
    quarters = chunks // 2
    ranks = tiles // chunks
    me_chunk = lax.rem(me_period, chunks)

    def rows_at(number, rows=ROWS, pitch=ROWS):
        return pl.ds(pl.multiple_of(number * pitch, ROWS), rows)

    def tile(ref, number):
        return ref[rows_at(number), :]

    def put(ref, number, values):
        ref[rows_at(number), :] = values

    def lanes_of(ref, number):
        return jnp.broadcast_to(ref[pl.ds(number, 1), :], (ROWS, LANES))

    loads = [
        pltpu.make_async_copy(source, target_ref, in_sem.at[k])
        for k, (source, target_ref) in enumerate(
            (
                (keep_in, keep),
                (dual_in, dual),
                (cut_tail_in, cut_tail),
                (cut_head_in, cut_head),
                (cut_in, cut),
                (cost_cut_in, cost_cut),
                (tail_in, tail),
                (head_in, head),
                (target_in, target),
                (cost_prod_in, cost_prod),
                (cost_inner_in, cost_inner),
                (flow_in, flow),
                (prod_in, prod),
            )
        )
    ]
    def greet(device):
        pl.semaphore_signal(
            pltpu.get_barrier_semaphore(), inc=1, device_id=device, device_id_type=MESH
        )

    def around(i):
        return lax.rem(
            me_period + periods // 2 + (1 - 2 * lax.rem(i, 2)) * lax.div(i + 1, 2), periods
        )

    def away(i):
        return lax.rem(2 + i + lax.div(i, 2) + 2 * lax.div(i, 3), 4)

    def across(k):
        y = lax.rem(lax.div(me_node, 8) + away(lax.div(k, 8)), 4)
        x = lax.rem(lax.div(me_node, 2) + away(lax.rem(lax.div(k, 2), 4)), 4)
        return y * 8 + x * 2 + lax.rem(me_node + 1 + k, 2)

    def greet_period(k, _):
        greet({"period": around(k)})
        return 0

    def greet_node(k, _):
        greet({"node": across(k)})
        return 0

    node_chunk = lax.rem(me_node, chunks)

    for load in loads[:2]:
        load.start()
    lax.fori_loop(0, periods - 1, greet_period, 0)
    for load in loads[2:]:
        load.start()
    lax.fori_loop(0, nodes - 1, greet_node, 0)

    def start(source, target_ref, source_rows, target_rows, phase, device):
        pltpu.make_async_remote_copy(
            src_ref=source.at[source_rows, :],
            dst_ref=target_ref.at[target_rows, :],
            send_sem=send_sem.at[phase],
            recv_sem=recv_sem.at[phase],
            device_id=device,
            device_id_type=MESH,
        ).start()

    def spread_owners(source, target_ref, phase):
        def one(k, _):
            peer = around(k)
            start(
                source, target_ref, rows_at(lax.rem(peer, chunks)), rows_at(me_period), phase, {"period": peer}
            )
            return 0

        lax.fori_loop(0, periods - 1, one, 0)
        put(target_ref, me_period, tile(source, me_chunk))

    def give(source, count, own_ref, phase, far_ref=None, far_phase=None):
        place = lax.rem(me_period, count)

        def one(i, _):
            pair = lax.div(i, 2)
            peer = lax.rem(
                me_period + periods - count // 2 + pair + lax.rem(i, 2) * (count - 1 - 2 * pair), periods
            )
            if far_ref is not None:
                for rank in range(ranks):
                    to = me_chunk + rank * chunks

                    @pl.when(to != me_node)
                    def _():
                        start(
                            source, far_ref,
                            pl.ds(pl.multiple_of(peer * ROWS, ROWS) + 2 * rank, 2), rows_at(me_node, 2), far_phase,
                            {"node": to, "period": peer},
                        )

            @pl.when(peer != me_period)
            def _():
                start(source, own_ref, rows_at(peer), rows_at(place), phase, {"period": peer})

            return 0

        lax.fori_loop(0, count, one, 0)
        put(own_ref, place, tile(source, me_period))

    def spread_nodes(source, target_ref, pitch, rows, phase, same=False):
        def one(k, _):
            peer = across(k)
            start(
                source, target_ref, rows_at(0 if same else peer, rows, pitch), rows_at(me_node, rows, pitch), phase,
                {"node": peer},
            )
            return 0

        lax.fori_loop(0, nodes - 1, one, 0)

    def await_rows(ref, rows, semaphore):
        span = ref.at[pl.ds(0, rows), :]
        pltpu.make_async_copy(span, span, semaphore).wait()

    def put_summary(ref, row, values):
        for rank in range(ranks):
            ref[pl.ds(2 * rank + row, chunks, stride=ROWS), :] = values[rank * chunks : (rank + 1) * chunks]

    def get_summary(ref, row):
        return jnp.concatenate(
            [ref[pl.ds(2 * rank + row, chunks, stride=ROWS), :] for rank in range(ranks)], axis=0
        )

    def put_quarters(ref, values):
        for row in range(2 * ranks):
            ref[pl.ds(row, quarters, stride=ROWS), :] = values[row * quarters : (row + 1) * quarters]

    def get_quarters(ref):
        return jnp.concatenate(
            [ref[pl.ds(row, quarters, stride=ROWS), :] for row in range(2 * ranks)], axis=0
        )

    def at_period(ref, t):
        return ref[pl.ds(t * tiles, tiles), :]

    def by_node(ref, t, pitch=ROWS):
        return ref[pl.ds(t, tiles, stride=pitch), :]

    def chain_back(values, shares, entering, target_ref):
        for t in reversed(range(ROWS)):
            entering = values(t) + entering
            target_ref[pl.ds(t, tiles, stride=ROWS), :] = entering * (1.0 / horizon)
            entering = entering * at_period(shares, t)

    def passed_back():
        passed = None
        for t in reversed(range(ROWS)):
            value = at_period(duals, t)
            passed = value if passed is None else value + passed
            passed = passed * at_period(kept, t)
        return passed

    def products(share_of, shares, target_ref):
        product = None
        square_sum = None
        for t in range(ROWS):
            share = share_of(t)
            shares[pl.ds(t * tiles, tiles), :] = share
            product = share if product is None else product * share
            target_ref[pl.ds(t * tiles, tiles), :] = product
            square = product * product
            square_sum = square if square_sum is None else square_sum + square
        return product, square_sum

    even = (lax.broadcasted_iota(jnp.int32, (ROWS, LANES), 0) & 1) == 0
    none = jnp.zeros((ROWS, LANES), jnp.float32)

    loads[0].wait()
    loads[1].wait()
    product, square_sum = products(lambda t: by_node(keep, t), kept, grown)
    for t in range(ROWS):
        duals[pl.ds(t * tiles, tiles), :] = by_node(dual, t)
    put_summary(send_a, 0, product)
    put_summary(send_a, 1, passed_back())
    put_summary(send_s, 1, square_sum)
    put_summary(
        send_s,
        0,
        jnp.concatenate(
            [
                pltpu.roll(product[rank * chunks : (rank + 1) * chunks], quarters, 0)
                for rank in range(ranks)
            ],
            axis=0,
        ),
    )

    for k in (2, 3, 4, 5):
        loads[k].wait()

    def pack_one(step, _):
        for k in range(UNROLL):
            d = step * UNROLL + k
            for place, ref in enumerate((cut, cost_cut, keep, dual)):
                pack[rows_at(d * (PACK // ROWS) + place), :] = tile(ref, d)
        return 0

    lax.fori_loop(0, nodes // UNROLL, pack_one, 0)
    cut_tail[...] = cut_tail[...] & (LANES - 1)
    cut_head[...] = cut_head[...] & (LANES - 1)
    pack[pl.ds(4 * ROWS, nodes, stride=PACK), :] = cut_tail[...].astype(jnp.float32)
    pack[pl.ds(4 * ROWS + 1, nodes, stride=PACK), :] = cut_head[...].astype(jnp.float32)

    for k in (8, 9, 10):
        loads[k].wait()

    def square_one(t, sums):
        costs, wanted = sums
        value = tile(target, t)
        wanted = wanted + value * value
        value = tile(cost_prod, t)
        first = value * value
        value = tile(cost_cut, t)
        other = value * value
        for group in range(groups):
            value = tile(cost_inner, group * tiles + t)
            if group % 2:
                first = first + value * value
            else:
                other = other + value * value
        return costs + (first + other), wanted

    costs, wanted = lax.fori_loop(0, tiles, square_one, (none, none))
    first_row = lax.broadcasted_iota(jnp.int32, (ROWS, LANES), 0) < 1
    part[...] = jnp.where(
        first_row, jnp.sum(costs, axis=0, keepdims=True), jnp.sum(wanted, axis=0, keepdims=True)
    )

    pl.semaphore_wait(pltpu.get_barrier_semaphore(), periods + nodes - 2)
    spread_owners(send_a, recv_a, 0)
    spread_nodes(part, parts, ROWS, 2, 5, same=True)
    put(parts, me_node, part[...])
    spread_nodes(pack, packs, PACK, SENT, 2)

    loads[6].wait()
    loads[7].wait()
    tail[...] = tail[...] & (LANES - 1)
    head[...] = head[...] & (LANES - 1)

    def keyed(first, other):
        lane = lax.broadcasted_iota(jnp.int32, first.shape, 1)
        return (first * (LANES * LANES) + other * LANES + lane).astype(jnp.float32)

    keys[pl.ds(0, blocks), :] = keyed(tail[...], head[...])
    keys[pl.ds(blocks, blocks), :] = keyed(head[...], tail[...])
    keys[pl.ds(2 * blocks, nodes), :] = keyed(cut_tail[...], cut_head[...])
    keys[pl.ds(2 * blocks + nodes, nodes), :] = keyed(cut_head[...], cut_tail[...])
    batch = 2 * blocks + 2 * nodes

    def sort_batch(k, _):
        at = pl.ds(pl.multiple_of(k * batch, batch), batch)
        ordered = sort_lanes(keys[at, :]).astype(jnp.int32)
        second[at, :] = lax.shift_right_logical(ordered, 7) & (LANES - 1)
        slot[at, :] = ordered & (LANES - 1)
        return 0

    lax.fori_loop(0, (2 * blocks + 2 * nodes) // batch, sort_batch, 0)

    loads[11].wait()
    loads[12].wait()

    def reorder(step, _):
        moved = []
        for k in range(UNROLL):
            t = step * UNROLL + k
            for group in range(groups):
                j = group * tiles + t
                lanes = lanes_of(slot, j)
                moved.append((flow, j, take(tile(flow, j), lanes)))
                moved.append((cost_inner, j, take(tile(cost_inner, j), lanes)))
            lanes = lanes_of(slot, 2 * blocks + t)
            moved.append((cut, t, take(tile(cut, t), lanes)))
            moved.append((cost_cut, t, take(tile(cost_cut, t), lanes)))
        for ref, number, values in moved:
            put(ref, number, values)
        return 0

    lax.fori_loop(0, tiles // UNROLL, reorder, 0)
    for t in range(ROWS):
        targets[pl.ds(t * tiles, tiles), :] = by_node(target, t)

    await_rows(parts, (nodes - 1) * 2, recv_sem.at[5])
    whole[...] = jnp.where(
        first_row,
        jnp.sum(parts[pl.ds(0, nodes, stride=ROWS), :], axis=0, keepdims=True),
        jnp.sum(parts[pl.ds(1, nodes, stride=ROWS), :], axis=0, keepdims=True),
    )

    def spread_whole(k, _):
        start(whole, wholes, rows_at(0, 2), rows_at(me_period, 2), 12, {"period": around(k)})
        return 0

    lax.fori_loop(0, periods - 1, spread_whole, 0)
    put(wholes, me_period, whole[...])

    await_rows(recv_a, (periods - 1) * ROWS, recv_sem.at[0])
    entering = none
    for j in reversed(range(periods)):
        block = tile(recv_a, j)
        ratio = jnp.where(even, block, pltpu.roll(block, 1, 0))
        put(factor, j, ratio)
        put(give_a, j, entering)
        entering = block + ratio * entering
    give(give_a, chunks, got_a, 3, far_a, 4)

    await_rows(packs, (nodes - 1) * SENT, recv_sem.at[2])
    packs[rows_at(me_node, PACK, PACK), :] = pack[rows_at(me_node, PACK, PACK), :]
    ends_out[...] = take(
        packs[pl.ds(4 * ROWS + 1, nodes, stride=PACK), :], slot[pl.ds(2 * blocks, nodes), :]
    ).astype(jnp.int32)
    ends_in[...] = take(
        packs[pl.ds(4 * ROWS, nodes, stride=PACK), :], slot[pl.ds(2 * blocks + nodes, nodes), :]
    ).astype(jnp.int32)

    def reorder_back(step, _):
        moved = []
        for k in range(UNROLL):
            d = step * UNROLL + k
            lanes = lanes_of(slot, 2 * blocks + nodes + d)
            for place, ref in enumerate((flow_back, cost_back)):
                moved.append((ref, d, take(tile(packs, d * (PACK // ROWS) + place), lanes)))
        for ref, number, values in moved:
            put(ref, number, values)
        return 0

    lax.fori_loop(0, nodes // UNROLL, reorder_back, 0)
    products(lambda t: packs[pl.ds(2 * ROWS + t, nodes, stride=PACK), :], kept_far, grown_far)

    def update_inner(tau):
        def one(step, _):
            stores = []
            for k in range(UNROLL):
                t = step * UNROLL + k
                here = tile(price, t)
                old = tile(prod, t)
                new = jnp.maximum(old - tau * (tile(cost_prod, t) - here), 0.0)
                stores.append((prod, t, new))
                total = 2.0 * new - old
                for group in range(groups):
                    j = group * tiles + t
                    there = take(tile(price, lax.rem(t + group, tiles)), lanes_of(second, j))
                    old = tile(flow, j)
                    new = jnp.maximum(old - tau * (tile(cost_inner, j) - (there - here)), 0.0)
                    moved = 2.0 * new - old
                    stores.append((flow, j, new))
                    stores.append((change, j, moved))
                    total = total - moved
                stores.append((net, t, total))
            for ref, number, values in stores:
                put(ref, number, values)
            return 0

        lax.fori_loop(0, tiles // UNROLL, one, 0)

    def gather_inner():
        def one(step, _):
            stores = []
            for k in range(UNROLL):
                t = step * UNROLL + k
                total = tile(net, t)
                for group in range(groups):
                    j = group * tiles + lax.rem(t - group + tiles, tiles)
                    total = total + take(tile(change, j), lanes_of(second, blocks + j))
                stores.append((net, t, total))
            for ref, number, values in stores:
                put(ref, number, values)
            return 0

        lax.fori_loop(0, tiles // UNROLL, one, 0)

    def update_cut(tau):
        put(price_far, me_node, tile(price, me_node))

        def one(step, _):
            stores = []
            for k in range(UNROLL):
                t = step * UNROLL + k
                here = tile(price, t)
                other = tile(price_far, t)
                there = take(other, lanes_of(ends_out, t))
                old = tile(cut, t)
                new = jnp.maximum(old - tau * (tile(cost_cut, t) - (there - here)), 0.0)
                stores.append((cut, t, new))
                total = tile(net, t) - (2.0 * new - old)
                there = take(other, lanes_of(ends_in, t))
                old = tile(flow_back, t)
                new = jnp.maximum(old - tau * (tile(cost_back, t) - (here - there)), 0.0)
                stores.append((flow_back, t, new))
                stores.append((net, t, total + (2.0 * new - old)))
            for ref, number, values in stores:
                put(ref, number, values)
            return 0

        lax.fori_loop(0, tiles // UNROLL, one, 0)

    await_rows(got_a, (chunks - 1) * ROWS, recv_sem.at[3])
    chain_back(lambda t: at_period(duals, t), kept, get_summary(got_a, 1), price)
    spread_owners(send_s, recv_s, 1)
    await_rows(wholes, (periods - 1) * 2, recv_sem.at[12])
    sums = [jnp.sum(wholes[pl.ds(row, periods, stride=ROWS), :], keepdims=True) for row in range(2)]
    omega = jnp.sqrt(sums[0] / sums[1])
    tau = jnp.broadcast_to(ETA / omega, (ROWS, LANES))
    sigma = ETA * omega
    sigma_tile = jnp.broadcast_to(sigma, (ROWS, LANES)) * (1.0 / horizon)
    sigma_wide = jnp.broadcast_to(sigma, (tiles, LANES))
    sigma_stock = sigma_wide * (1.0 / horizon)
    update_inner(tau)
    gather_inner()
    await_rows(far_a, (nodes - 1) * 2, recv_sem.at[4])
    chain_back(
        lambda t: packs[pl.ds(3 * ROWS + t, nodes, stride=PACK), :], kept_far, by_node(far_a, 1), price_far
    )
    update_cut(tau)

    def local_stock(target_ref):
        stock = None
        for t in range(ROWS):
            value = by_node(net, t)
            stock = value if stock is None else at_period(kept, t) * stock + value
            value = at_period(duals, t) + sigma_wide * (at_period(targets, t) - stock * (1.0 / horizon))
            duals[pl.ds(t * tiles, tiles), :] = value
            if target_ref is not None:
                target_ref[pl.ds(t, tiles, stride=ROWS), :] = value
        return stock

    put_summary(send_b, 0, local_stock(late))
    put_summary(send_b, 1, passed_back())
    spread_owners(send_b, recv_b, 6)
    spread_nodes(late, lates, ROWS, ROWS, 7)
    await_rows(recv_s, (periods - 1) * ROWS, recv_sem.at[1])
    for j in range(periods):
        other = tile(recv_s, j)
        ratio = tile(factor, j)
        low = jnp.where(even, ratio, pltpu.roll(other, 1, 0))
        put(factor_c, j, jnp.where(me_chunk < quarters, low, jnp.where(even, other, ratio)))

    await_rows(recv_b, (periods - 1) * ROWS, recv_sem.at[6])
    entering = none
    entered = []
    for j in range(periods):
        entered.append(entering)
        entering = tile(recv_b, j) + tile(factor, j) * entering
    entering = none
    for j in reversed(range(periods)):
        put(give_b, j, jnp.where(even, entered[j], entering))
        answer = tile(recv_b, j) - sigma_tile * tile(recv_s, j) * pltpu.roll(entered[j], 1, 0)
        entering = answer + tile(factor, j) * entering
    give(give_b, chunks, got_b, 8, far_b, 9)

    await_rows(got_b, (chunks - 1) * ROWS, recv_sem.at[8])
    stock = get_summary(got_b, 0) * sigma_stock
    for t in range(ROWS):
        duals[pl.ds(t * tiles, tiles), :] = at_period(duals, t) - at_period(grown, t) * stock
    chain_back(lambda t: at_period(duals, t), kept, get_summary(got_b, 1), price)
    update_inner(tau)
    gather_inner()
    await_rows(lates, (nodes - 1) * ROWS, recv_sem.at[7])
    await_rows(far_b, (nodes - 1) * 2, recv_sem.at[9])
    stock_far = by_node(far_b, 0) * sigma_stock
    chain_back(
        lambda t: by_node(lates, t) - at_period(grown_far, t) * stock_far, kept_far, by_node(far_b, 1), price_far
    )
    update_cut(tau)
    put_quarters(send_c, local_stock(None))

    def spread_later(k, _):
        peer = around(k)

        @pl.when(jnp.logical_and(me_period < periods - 1, jnp.logical_or(me_period < peer, peer < 2)))
        def _():
            pltpu.make_async_remote_copy(
                src_ref=send_c.at[rows_at(lax.rem(peer, quarters)), :],
                dst_ref=recv_c.at[rows_at(me_period), :],
                send_sem=send_sem_c.at[peer],
                recv_sem=recv_sem_c.at[me_period],
                device_id={"period": peer},
                device_id_type=MESH,
            ).start()

        return 0

    lax.fori_loop(0, periods - 1, spread_later, 0)
    put(recv_c, me_period, tile(send_c, lax.rem(me_period, quarters)))

    def restore(step, _):
        moved = []
        for k in range(UNROLL):
            t = step * UNROLL + k
            for group in range(groups):
                j = group * tiles + t
                moved.append((flow, j, take(tile(flow, j), lanes_of(tail, j))))
            moved.append((cut, t, take(tile(cut, t), lanes_of(cut_tail, t))))
        for ref, number, values in moved:
            put(ref, number, values)
        return 0

    lax.fori_loop(0, tiles // UNROLL, restore, 0)

    def await_earlier(j, _):
        @pl.when(
            jnp.logical_and(
                jnp.logical_and(j < periods - 1, j != me_period),
                jnp.logical_or(j < me_period, me_period < 2),
            )
        )
        def _():
            await_rows(packs, ROWS, recv_sem_c.at[j])

        return 0

    lax.fori_loop(0, periods, await_earlier, 0)
    entering = none
    for j in range(periods):
        put(give_c, j, entering)
        entering = tile(recv_c, j) + tile(factor_c, j) * entering
    give(give_c, quarters, got_c, 11)
    await_rows(got_c, (quarters - 1) * ROWS, recv_sem.at[11])
    stock = get_quarters(got_c) * sigma_stock
    for t in range(ROWS):
        dual[pl.ds(t, tiles, stride=ROWS), :] = at_period(duals, t) - at_period(grown, t) * stock

    for phase, rows in (
        (0, (periods - 1) * ROWS),
        (1, (periods - 1) * ROWS),
        (2, (nodes - 1) * SENT),
        (3, (chunks - 1) * ROWS),
        (5, (nodes - 1) * 2),
        (12, (periods - 1) * 2),
        (6, (periods - 1) * ROWS),
        (7, (nodes - 1) * ROWS),
        (8, (chunks - 1) * ROWS),
        (11, (quarters - 1) * ROWS),
    ):
        await_rows(packs, rows, send_sem.at[phase])

    def await_sent(k, _):
        peer = around(k)

        @pl.when(jnp.logical_and(me_period < periods - 1, jnp.logical_or(me_period < peer, peer < 2)))
        def _():
            await_rows(packs, ROWS, send_sem_c.at[peer])

        return 0

    lax.fori_loop(0, periods - 1, await_sent, 0)
    for phase in (4, 9):
        await_rows(packs, chunks * (ranks - 1) * 2, send_sem.at[phase])

        @pl.when(me_chunk != node_chunk)
        def _():
            await_rows(packs, chunks * 2, send_sem.at[phase])


def hand_over(count, *refs):
    semaphores = refs[-1]
    copies = [
        pltpu.make_async_copy(refs[k], refs[count + k], semaphores.at[k]) for k in range(count)
    ]
    for copy in copies:
        copy.start()
    for copy in copies:
        copy.wait()


def solution(mesh):
    nodes, periods = mesh.shape["node"], mesh.shape["period"]

    def to_tiles(values):
        rows, columns = values.shape
        return values.reshape(rows, columns // LANES, LANES).transpose(1, 0, 2).reshape(-1, LANES)

    def from_tiles(values):
        count = values.shape[0] // ROWS
        return values.reshape(count, ROWS, LANES).transpose(1, 0, 2).reshape(ROWS, count * LANES)

    def body(*operands):
        floats = [to_tiles(values) for values in operands[:9]]
        indices = [values.reshape(-1, LANES) for values in operands[9:]]
        tiles = floats[0].shape[0] // ROWS
        groups = floats[1].shape[0] // floats[0].shape[0]
        blocks = tiles * groups
        slab = (tiles * ROWS, LANES)
        arcs = (blocks * ROWS, LANES)
        ring = (periods * ROWS, LANES)
        sorts = (2 * blocks + 2 * nodes, LANES)

        def room(shape, kind=jnp.float32):
            return pltpu.VMEM(shape, kind)

        scratch = [
            room(slab), room(arcs), room(slab), room(slab), room(slab),
            room((blocks, LANES), jnp.int32), room((blocks, LANES), jnp.int32),
            room((tiles, LANES), jnp.int32), room((tiles, LANES), jnp.int32),
            room(slab), room(slab), room(slab), room(slab), room(slab), room(slab),
            room(slab), room(slab), room(slab), room(arcs),
            room(sorts), room(sorts, jnp.int32), room(sorts, jnp.int32),
            room((nodes, LANES), jnp.int32), room((nodes, LANES), jnp.int32),
            room((nodes * PACK, LANES)), room((nodes * PACK, LANES)), room(slab), room(slab),
            room(slab), room(slab), room((ROWS, LANES)), room(slab), room((ROWS, LANES)), room(ring),
            room(ring), room(ring), room(ring), room(ring), room(slab), room(ring), room(ring),
            room(ring), room(ring), room(ring), room(ring), room(slab),
            room(ring), room(ring), room(ring), room(ring),
            room(ring), room(ring),
            pltpu.SemaphoreType.DMA((13,)),
            pltpu.SemaphoreType.DMA((13,)),
            pltpu.SemaphoreType.DMA((13,)),
            pltpu.SemaphoreType.DMA((periods,)),
            pltpu.SemaphoreType.DMA((periods,)),
        ]
        anywhere = pl.BlockSpec(memory_space=pl.ANY)
        inside = pl.BlockSpec(memory_space=pltpu.VMEM)
        shapes = (slab, arcs, slab, slab)
        results = pl.pallas_call(
            functools.partial(kernel, (nodes, periods, tiles, groups)),
            out_shape=[pltpu.VMEM(shape, jnp.float32) for shape in shapes],
            in_specs=[anywhere] * 13,
            out_specs=[inside] * 4,
            scratch_shapes=scratch,
            compiler_params=pltpu.CompilerParams(
                collective_id=0, has_side_effects=True, vmem_limit_bytes=LIMIT
            ),
        )(*floats, *indices)
        outputs = pl.pallas_call(
            functools.partial(hand_over, 4),
            out_shape=[jax.ShapeDtypeStruct(shape, jnp.float32) for shape in shapes],
            in_specs=[anywhere] * 4,
            out_specs=[anywhere] * 4,
            scratch_shapes=[pltpu.SemaphoreType.DMA((4,))],
            compiler_params=pltpu.CompilerParams(vmem_limit_bytes=LIMIT // 8),
        )(*results)
        return tuple(from_tiles(values) for values in outputs)

    both, node = P("period", "node"), P("node")
    return jax.shard_map(
        body,
        mesh=mesh,
        in_specs=(both,) * 9 + (node,) * 4,
        out_specs=(both,) * 4,
        check_vma=False,
    )
```
